256 devices in a mesh: req: 8 (over z), shard: 32 (over x, y, core).
Axes of the slice: x: 4, y: 4, z: 8, core: 2. Of those that a mesh axis runs over, the one named last changes fastest.
Arguments:
- paged_key_store: bfloat16 [2816, 16, 1024], P(('req', 'shard')), parts along dimension 0, may hold values from -6 to 6
- paged_value_store: bfloat16 [2816, 16, 1024], P(('req', 'shard')), parts along dimension 0, may hold values from -6 to 6
- paged_scale_store: float32 [2816, 2, 8], P(('req', 'shard')), parts along dimension 0, may hold values from 0.5 to 2
- page_map: int32 [2816], P('req'), parts along dimension 0, may hold values from 0 to 351, each once
- span_order: int32 [64], P('req'), parts along dimension 0, may hold values from 0 to 7, each once
- listed_count: int32 [256], P('req'), parts along dimension 0, may hold values from 4 to 48, as said below
- listed_index: int32 [12288], P('req'), parts along dimension 0, may hold values from 0 to 175, as said below
- listed_queries: bfloat16 [12288, 8192], P(('req', 'shard')), parts along dimension 0, may hold values from -440 to 440
- selected_token_keys: bfloat16 [12288, 1024], P(('req', 'shard')), parts along dimension 0, may hold values from -4.25 to 4.25
- selected_token_values: bfloat16 [12288, 1024], P(('req', 'shard')), parts along dimension 0, may hold values from -6 to 6
Outputs:
- mixed_cache_keys: bfloat16 [2816, 16, 1024], P(('req', 'shard')), parts along dimension 0
- mixed_cache_values: bfloat16 [2816, 16, 1024], P(('req', 'shard')), parts along dimension 0
- attended: bfloat16 [12288, 8192], P(('req', 'shard')), parts along dimension 0
The draws below stay inside these ranges and needn't reach their ends.
There are 8 independent parts, one for each index of `req`. The reference program is written for one: setup_inputs(seed, part) draws one part's arguments, and reference() takes and returns one part's arrays. A program takes and returns all parts, laid end to end along the dimension named above; each array names one. Nothing has to cross between parts.
Inputs may be any that keep to these rules, and one draw needn't show every extreme that they name: `listed_count`: at least 4 on every token shard, exactly 48 on some shard, 26 per shard on average. `listed_index`: the 48 entries of one token shard are distinct; only the first listed_count of them are listed.
All inputs are finite; a program needn't handle non-finite values.
Results may differ from the reference program's by a relative error of at most 0.006.
The reference program's roundings to bfloat16 on the way count: a program that leaves them out, or rounds other values in their place, can miss the bound.
Values may be sent and summed in bfloat16 or wider, within the bound.
No kernel may reach another device: no remote copies, remote signals or barrier semaphores. Data moves between devices by JAX's collectives and lax.ppermute only.
A program may use at most 128 MiB of HBM per device.

```python
import math
import jax
import jax.numpy as jnp
from jax import lax

QUERY_HEADCOUNT = 64
KEY_VALUE_HEADS = 8
HEAD_DIMENSION = 128
PAGE_TOKENS = 16
SPAN_LEN = 704
TOK_DEV = 176
STORED_PAGES = 352
SPANS = 8
LIST_DEV = 26
SHARD_TOKEN_LIMIT = 48
N_SHARD = 32


def draw_listed_count(key, part):
    key = jax.random.fold_in(key, 11)
    leading_key_half, trailing_key_half = jax.random.split(key)
    shuffled = jax.random.permutation(leading_key_half, N_SHARD)
    moves = jax.random.randint(trailing_key_half, (N_SHARD // 2,), 0, LIST_DEV - 3)
    moves = moves.at[0].set(LIST_DEV - 4)
    gains = jnp.stack([moves, -moves], axis=1).reshape(-1)
    counts = jnp.zeros((N_SHARD,), jnp.int32).at[shuffled].set(LIST_DEV + gains)
    return counts.astype(jnp.int32)


def draw_listed_index(key, part):
    key = jax.random.fold_in(key, 12)
    scores = jax.random.randint(key, (N_SHARD, TOK_DEV), 0, 1 << 16) * TOK_DEV + jnp.arange(TOK_DEV, dtype=jnp.int32)[None, :]
    ordered = jnp.argsort(scores, axis=1, stable=True)
    return ordered[:, :SHARD_TOKEN_LIMIT].reshape(-1).astype(jnp.int32)


def draw_selected_token_keys(key, part):
    key = jax.random.fold_in(key, 13)
    unrotated_keys = jnp.clip(jax.random.normal(key, (N_SHARD * SHARD_TOKEN_LIMIT, KEY_VALUE_HEADS, HEAD_DIMENSION), jnp.float32), -4.0, 4.0)
    return unrotated_keys.reshape(N_SHARD * SHARD_TOKEN_LIMIT, KEY_VALUE_HEADS * HEAD_DIMENSION).astype(jnp.bfloat16)


def draw_listed_queries(key, part):
    key = jax.random.fold_in(key, 14)
    unrotated_keys = jnp.clip(jax.random.normal(key, (N_SHARD * SHARD_TOKEN_LIMIT, QUERY_HEADCOUNT, HEAD_DIMENSION), jnp.float32), -4.0, 4.0)
    return unrotated_keys.reshape(N_SHARD * SHARD_TOKEN_LIMIT, QUERY_HEADCOUNT * HEAD_DIMENSION).astype(jnp.bfloat16)


def block_scale(rng, dims, cuts, low, largest):
    def one(dim, blocks):
        steps = jax.random.uniform(jax.random.fold_in(jax.random.fold_in(rng, 6), dim), (blocks,), jnp.float32, low / len(cuts), largest / len(cuts))
        return jnp.repeat(jnp.exp(steps), dims[dim] // blocks).reshape((-1,) + (1,) * (len(dims) - dim - 1))

    level = one(*cuts[0])
    for cut in cuts[1:]:
        level = level * one(*cut)
    return level


def bell_draw(stream_key, dims, spread, most, cuts=(), held_as=jnp.bfloat16):
    array = jax.random.normal(stream_key, dims, jnp.float32) * spread
    if len(cuts) > 0:
        array = block_scale(stream_key, dims, cuts, -0.22, 0.18) * array
    return jnp.clip(array, min=-most, max=most).astype(held_as)


def setup_inputs(seed: int = 0, part: int = 0) -> dict:
    streams_of = jax.random.split(jax.random.key(seed), 11)
    part_splits = jax.random.split(jax.random.fold_in(streams_of[10], part), 11)
    paged_key_store = bell_draw(part_splits[0], (STORED_PAGES, PAGE_TOKENS, KEY_VALUE_HEADS * HEAD_DIMENSION), 1.0, 6.0, ((0, 32),))
    paged_value_store = bell_draw(part_splits[1], (STORED_PAGES, PAGE_TOKENS, KEY_VALUE_HEADS * HEAD_DIMENSION), 1.0, 6.0, ((0, 32),))
    paged_scale_store = jnp.clip(jnp.exp(math.log(2.0) - 1.3862944 * jax.random.uniform(part_splits[2], (STORED_PAGES, 2, KEY_VALUE_HEADS), jnp.float32) ** block_scale(part_splits[2], (STORED_PAGES, 2, KEY_VALUE_HEADS), ((0, 32),), -0.2, 0.2)), 0.5, 2.0)
    page_map = jax.random.permutation(part_splits[3], STORED_PAGES).astype(jnp.int32)
    span_order = jax.random.permutation(part_splits[4], SPANS).astype(jnp.int32)
    listed_count = draw_listed_count(jax.random.fold_in(jax.random.fold_in(streams_of[10], part), 71), part)
    listed_index = draw_listed_index(jax.random.fold_in(jax.random.fold_in(streams_of[10], part), 71), part)
    listed_queries = draw_listed_queries(jax.random.fold_in(jax.random.fold_in(streams_of[10], part), 71), part)
    selected_token_keys = draw_selected_token_keys(jax.random.fold_in(jax.random.fold_in(streams_of[10], part), 71), part)
    selected_token_values = bell_draw(part_splits[9], (N_SHARD * SHARD_TOKEN_LIMIT, KEY_VALUE_HEADS * HEAD_DIMENSION), 1.0, 6.0, ((0, 32),))
    return dict(paged_key_store=paged_key_store, paged_value_store=paged_value_store, paged_scale_store=paged_scale_store, page_map=page_map, span_order=span_order, listed_count=listed_count, listed_index=listed_index, listed_queries=listed_queries, selected_token_keys=selected_token_keys, selected_token_values=selected_token_values)


rope_base = 1000000.0


def apply_rotation(vectors, position):
    half_size = vectors.shape[-1] // 2
    frequency = rope_base ** (-(jnp.arange(half_size, dtype=jnp.float32) * 2.0) / vectors.shape[-1])
    angles = position[..., None].astype(jnp.float32) * frequency
    cosine = jnp.cos(angles)
    sine_part = jnp.sin(angles)
    first_half = vectors[..., :half_size]
    second_half = vectors[..., half_size:]
    return jnp.concatenate([first_half * cosine - second_half * sine_part, second_half * cosine + first_half * sine_part], axis=-1)


def layout_tables(page_map, span_order, listed_count, listed_index, page_token_count, span_size, shard_tokens):
    stored_page_count = page_map.shape[0]
    span_count = span_order.shape[0]
    per_span = span_size // page_token_count
    shard_count = listed_count.shape[0]
    row_cap = listed_index.shape[0] // shard_count
    logical = jnp.zeros((stored_page_count,), jnp.int32).at[page_map].set(jnp.arange(stored_page_count, dtype=jnp.int32))
    slot_of = jnp.zeros((span_count,), jnp.int32).at[span_order].set(jnp.arange(span_count, dtype=jnp.int32))
    row_shift = slot_of[logical // per_span] * span_size
    row_start = row_shift + (logical % per_span) * page_token_count
    key_position = (row_start[:, None] + jnp.arange(page_token_count, dtype=jnp.int32)[None, :]).reshape(-1)
    selected_token_position = (jnp.arange(shard_count, dtype=jnp.int32)[:, None] * shard_tokens + listed_index.reshape(shard_count, row_cap)).reshape(-1)
    listed_valid = (jnp.arange(row_cap, dtype=jnp.int32)[None, :] < listed_count[:, None]).reshape(-1)
    span_slot = selected_token_position // span_size
    within_span = selected_token_position % span_size
    stored_row = page_map[span_order[span_slot] * per_span + within_span // page_token_count]
    cache_index = stored_row * page_token_count + within_span % page_token_count
    return row_shift, key_position, selected_token_position, listed_valid, cache_index


def reference(paged_key_store, paged_value_store, paged_scale_store, page_map, span_order, listed_count, listed_index, listed_queries, selected_token_keys, selected_token_values):
    stored_page_count, page_token_count, key_value_width = paged_key_store.shape
    query_group_width = QUERY_HEADCOUNT // KEY_VALUE_HEADS
    row_shift, key_position, selected_token_position, listed_valid, cache_index = layout_tables(page_map, span_order, listed_count, listed_index, page_token_count, SPAN_LEN, TOK_DEV)
    dequantized_rows = paged_key_store.astype(jnp.float32).reshape(stored_page_count, page_token_count, KEY_VALUE_HEADS, HEAD_DIMENSION) * paged_scale_store[:, 0, None, :, None]
    cached_keys = apply_rotation(dequantized_rows, row_shift[:, None, None]).astype(jnp.bfloat16).reshape(-1, key_value_width)
    stored_value_rows = (paged_value_store.astype(jnp.float32).reshape(stored_page_count, page_token_count, KEY_VALUE_HEADS, HEAD_DIMENSION) * paged_scale_store[:, 1, None, :, None]).astype(jnp.bfloat16).reshape(-1, key_value_width)
    total_row_count = listed_queries.shape[0]
    recomputed_key_rows = apply_rotation(selected_token_keys.astype(jnp.float32).reshape(total_row_count, KEY_VALUE_HEADS, HEAD_DIMENSION), selected_token_position[:, None]).astype(jnp.bfloat16).reshape(total_row_count, key_value_width)
    query_rows = apply_rotation(listed_queries.astype(jnp.float32).reshape(total_row_count, QUERY_HEADCOUNT, HEAD_DIMENSION), selected_token_position[:, None]).astype(jnp.bfloat16)
    target = jnp.where(listed_valid, cache_index, cached_keys.shape[0])
    mixed_cache_keys = cached_keys.at[target].set(recomputed_key_rows, mode="drop")
    mixed_cache_values = stored_value_rows.at[target].set(selected_token_values, mode="drop")
    query_position = jnp.repeat(jnp.where(listed_valid, selected_token_position, -1), query_group_width)
    per_head_queries = query_rows.reshape(total_row_count, KEY_VALUE_HEADS, query_group_width, HEAD_DIMENSION).transpose(1, 0, 2, 3).reshape(KEY_VALUE_HEADS, total_row_count * query_group_width, HEAD_DIMENSION)
    per_head_keys = mixed_cache_keys.reshape(-1, KEY_VALUE_HEADS, HEAD_DIMENSION).transpose(1, 0, 2)
    per_head_values = mixed_cache_values.reshape(-1, KEY_VALUE_HEADS, HEAD_DIMENSION).transpose(1, 0, 2)
    score_scale = HEAD_DIMENSION ** -0.5

    def one_head(operands):
        these_queries, these_keys, these_values = operands
        scores = jnp.dot(these_queries, these_keys.T, preferred_element_type=jnp.float32) * score_scale
        visible = key_position[None, :] <= query_position[:, None]
        row_max = jnp.max(jnp.where(visible, scores, -1e30), axis=1, keepdims=True)
        exps = jnp.where(visible, jnp.exp(scores - row_max), 0.0)
        total = jnp.sum(exps, axis=1, keepdims=True)
        mixed = jnp.dot(exps.astype(jnp.bfloat16), these_values, preferred_element_type=jnp.float32)
        return mixed / jnp.where(total > 0, total, 1.0)

    attention_output = lax.map(one_head, (per_head_queries, per_head_keys, per_head_values))
    attended = attention_output.reshape(KEY_VALUE_HEADS, total_row_count, query_group_width, HEAD_DIMENSION).transpose(1, 0, 2, 3).reshape(total_row_count, QUERY_HEADCOUNT * HEAD_DIMENSION).astype(jnp.bfloat16)
    return mixed_cache_keys.reshape(paged_key_store.shape), mixed_cache_values.reshape(paged_value_store.shape), attended
```

```python
import functools

import jax
import jax.numpy as jnp
import numpy as np
from jax import lax
from jax.experimental import pallas as pl
from jax.experimental.pallas import tpu as pltpu
from jax.sharding import PartitionSpec as P

HEAD = 128
KV_HEADS = 8
SPAN_LEN = 704
ROPE_BASE = 1000000.0
MASKED = -1e30
EXP2_SCALE = float(HEAD**-0.5 / np.log(2.0))

BF16 = jnp.bfloat16
F32 = jnp.float32
I32 = jnp.int32
SMEM = pltpu.SMEM
VMEM = pltpu.VMEM


def rope_frequency():
    half = HEAD // 2
    frequency = ROPE_BASE ** (-(np.arange(half, dtype=np.float64) * 2.0) / HEAD)
    return np.concatenate([frequency, frequency]).astype(np.float32)[None, :]


def rope_tables(position, frequency):
    angles = position * frequency
    lane = lax.broadcasted_iota(I32, angles.shape, 1)
    sine = jnp.sin(angles)
    return jnp.cos(angles), jnp.where(lane < HEAD // 2, -sine, sine)


def rotate(x, cosine, sine):
    return x * cosine + pltpu.roll(x, HEAD // 2, 1) * sine


def params(mib, **more):
    return pltpu.CompilerParams(vmem_limit_bytes=mib * 1024 * 1024, **more)


def prepare_kv_kernel(
    shards,
    me_ref,
    page_map,
    span_order,
    listed_index,
    scale,
    frequency,
    keys,
    values,
    fresh_keys,
    fresh_values,
    out,
    cosine_out,
    sine_out,
    slots,
    positions,
    shift_cos,
    shift_sin,
):
    head = pl.program_id(0)
    me = me_ref[0]
    own_pages, page_tokens, _ = keys.shape
    rows = fresh_keys.shape[0]
    per_span = page_map.shape[0] // span_order.shape[0]
    span_count = span_order.shape[0]
    tokens = own_pages * page_tokens

    @pl.when(head == 0)
    def _():
        first = me * own_pages
        for slot in range(span_count):
            start = span_order[slot] * per_span

            def note(p, carry):
                place = page_map[start + p] - first
                inside = (place >= 0) & (place < own_pages)
                slots[jnp.where(inside, place, own_pages)] = slot
                return carry

            lax.fori_loop(0, per_span, note, 0, unroll=11)
        for c in range(rows):
            position = (me * tokens + listed_index[me * rows + c]).astype(F32)
            positions[c : c + 1, :] = jnp.full((1, HEAD), position, F32)
        cosine_out[...], sine_out[...] = rope_tables(positions[...], frequency[...])
        shift = lax.broadcasted_iota(I32, (span_count, HEAD), 0) * SPAN_LEN
        shift_cos[...], shift_sin[...] = rope_tables(shift.astype(F32), frequency[...])

    for page in range(own_pages):
        slot = slots[page]
        cosine = shift_cos[pl.ds(slot, 1), :]
        sine = shift_sin[pl.ds(slot, 1), :]
        span = slice(page * page_tokens, (page + 1) * page_tokens)
        key = keys[page].astype(F32) * scale[page, 0, head]
        key = rotate(key, cosine, sine).astype(BF16)
        value = (values[page].astype(F32) * scale[page, 1, head]).astype(BF16)
        out[0, span] = key
        out[1, span] = value
        out[2, span] = key
        out[3, span] = value
    key = rotate(fresh_keys[...].astype(F32), cosine_out[...], sine_out[...]).astype(BF16)
    value = fresh_values[...]
    out[0, tokens:] = key
    out[1, tokens:] = value
    out[2, tokens:] = key
    out[3, tokens:] = value


def prepare_kv(
    me, page_map, span_order, listed_index, scale, keys, values, fresh_keys, fresh_values, shards
):
    own_pages, page_tokens, _ = keys.shape
    rows = fresh_keys.shape[0]
    sent = own_pages * page_tokens + rows
    group = shards // KV_HEADS
    smem = pl.BlockSpec(memory_space=SMEM)
    return pl.pallas_call(
        functools.partial(prepare_kv_kernel, shards),
        grid=(KV_HEADS,),
        in_specs=[
            smem,
            smem,
            smem,
            smem,
            smem,
            pl.BlockSpec((1, HEAD), lambda h: (0, 0)),
            pl.BlockSpec((own_pages, page_tokens, HEAD), lambda h: (0, 0, h)),
            pl.BlockSpec((own_pages, page_tokens, HEAD), lambda h: (0, 0, h)),
            pl.BlockSpec((rows, HEAD), lambda h: (0, h)),
            pl.BlockSpec((rows, HEAD), lambda h: (0, h)),
        ],
        out_specs=[
            pl.BlockSpec((group, sent, HEAD), lambda h: (h, 0, 0)),
            pl.BlockSpec((rows, HEAD), lambda h: (0, 0)),
            pl.BlockSpec((rows, HEAD), lambda h: (0, 0)),
        ],
        out_shape=[
            jax.ShapeDtypeStruct((shards, sent, HEAD), BF16),
            jax.ShapeDtypeStruct((rows, HEAD), F32),
            jax.ShapeDtypeStruct((rows, HEAD), F32),
        ],
        scratch_shapes=[
            pltpu.SMEM((own_pages + 1,), I32),
            pltpu.VMEM((rows, HEAD), F32),
            pltpu.VMEM((span_order.shape[0], HEAD), F32),
            pltpu.VMEM((span_order.shape[0], HEAD), F32),
        ],
        compiler_params=params(24),
        cost_estimate=pl.CostEstimate(flops=4000000, bytes_accessed=2800000, transcendentals=0),
        name="prepare_kv",
    )(
        me,
        page_map,
        span_order,
        listed_index,
        scale,
        jnp.asarray(rope_frequency()),
        keys,
        values,
        fresh_keys,
        fresh_values,
    )


def prepare_queries_kernel(queries, cosine, sine, out):
    rows = cosine.shape[0]
    for j in range(out.shape[0]):
        for t in range(2):
            head = 2 * j + t
            x = queries[:, head * HEAD : (head + 1) * HEAD].astype(F32)
            out[j, t * rows : (t + 1) * rows] = rotate(x, cosine[...], sine[...]).astype(BF16)


def prepare_queries(queries, cosine, sine, shards):
    rows, width = queries.shape
    steps = 4
    return pl.pallas_call(
        prepare_queries_kernel,
        grid=(steps,),
        in_specs=[
            pl.BlockSpec((rows, width // steps), lambda h: (0, h)),
            pl.BlockSpec((rows, HEAD), lambda h: (0, 0)),
            pl.BlockSpec((rows, HEAD), lambda h: (0, 0)),
        ],
        out_specs=pl.BlockSpec((shards // steps, 2 * rows, HEAD), lambda h: (h, 0, 0)),
        out_shape=jax.ShapeDtypeStruct((shards, 2 * rows, HEAD), BF16),
        compiler_params=params(24),
        cost_estimate=pl.CostEstimate(flops=4000000, bytes_accessed=1600000, transcendentals=0),
        name="prepare_queries",
    )(queries, cosine, sine)


def plan_kernel(
    page_map,
    span_order,
    listed_count,
    listed_lanes,
    source,
    place,
    tiles,
    tile_count,
    positions,
    select,
):
    shards, wide = listed_lanes.shape
    tokens = select.shape[1]
    rows = wide - tokens
    own_pages = page_map.shape[0] // shards
    page_tokens = tokens // own_pages
    span_count = span_order.shape[0]
    per_span = page_map.shape[0] // span_count

    for slot in range(span_count):
        start = span_order[slot] * per_span

        def note(p, carry):
            stored = page_map[start + p]
            logical = slot * per_span + p
            owner = stored // own_pages
            source[logical] = owner * wide + (stored - owner * own_pages) * page_tokens
            place[stored] = logical * page_tokens
            return carry

        lax.fori_loop(0, per_span, note, 0, unroll=4)

    def list_tiles(shard, filled):
        count = listed_count[shard]
        for k in range(rows // 16):
            tiles[filled] = shard * (rows // 16) + k
            filled = filled + jnp.where(count > 16 * k, 1, 0)
        return filled

    filled = lax.fori_loop(0, shards, list_tiles, 0)
    tile_count[0] = filled
    last = tiles[filled - 1]

    def pad(k, carry):
        tiles[filled + k] = last
        return carry

    lax.fori_loop(0, 8, pad, 0)

    token = lax.broadcasted_iota(I32, (tokens, wide), 0)
    column = lax.broadcasted_iota(I32, (tokens, wide), 1)
    same = token == column
    row_of = lax.broadcasted_iota(I32, (rows, wide), 0) + tokens
    row_pick = row_of == lax.broadcasted_iota(I32, (rows, wide), 1)

    def fill(shard, carry):
        listed = listed_lanes[pl.ds(shard, 1), :]
        fresh = listed == token
        held = jnp.sum(jnp.where(fresh, 1.0, 0.0), axis=1, keepdims=True)
        cached = jnp.where(same, 1.0 - held, 0.0)
        select[shard] = jnp.where(fresh, 1.0, cached).astype(BF16)
        offset = jnp.sum(jnp.where(row_pick, listed.astype(F32), 0.0), axis=1, keepdims=True)
        position = jnp.where(offset < 0.0, -1.0, offset + (shard * tokens).astype(F32))
        start = pl.multiple_of(shard * rows, 16)
        positions[pl.ds(start, rows), :] = jnp.broadcast_to(position.astype(I32), (rows, HEAD))
        return carry

    lax.fori_loop(0, shards, fill, 0)


def plan(page_map, span_order, listed_count, listed_lanes, tokens):
    shards, wide = listed_lanes.shape
    rows = wide - tokens
    smem = pl.BlockSpec(memory_space=SMEM)
    vmem = pl.BlockSpec(memory_space=VMEM)
    pages = page_map.shape[0]
    tile_limit = shards * (rows // 16) + 8
    return pl.pallas_call(
        plan_kernel,
        in_specs=[smem, smem, smem, vmem],
        out_specs=[smem, smem, smem, smem, vmem, vmem],
        out_shape=[
            jax.ShapeDtypeStruct((pages,), I32),
            jax.ShapeDtypeStruct((pages,), I32),
            jax.ShapeDtypeStruct((tile_limit,), I32),
            jax.ShapeDtypeStruct((1,), I32),
            jax.ShapeDtypeStruct((shards * rows, HEAD), I32),
            jax.ShapeDtypeStruct((shards, tokens, wide), BF16),
        ],
        compiler_params=params(24),
        cost_estimate=pl.CostEstimate(flops=20000000, bytes_accessed=4000000, transcendentals=0),
        name="plan",
    )(page_map, span_order, listed_count, listed_lanes)


def blend_kernel(me_ref, source, place, select, received, ordered, returned):
    shards, wide, _ = received.shape
    tokens = select.shape[1]
    own_pages = source.shape[0] // shards
    page_tokens = tokens // own_pages
    flat = received.reshape(shards * wide, HEAD)

    def shard_step(shard, carry):
        pages = []
        for page in range(own_pages):
            start = pl.multiple_of(source[shard * own_pages + page], page_tokens)
            pages.append(flat[pl.ds(start, page_tokens), :])
        pages.append(received[shard, tokens:, :])
        start = pl.multiple_of(shard * tokens, 16)
        mixed = jnp.dot(
            select[shard], jnp.concatenate(pages, axis=0), preferred_element_type=F32
        )
        ordered[pl.ds(start, tokens), :] = mixed.astype(BF16)
        return carry

    lax.fori_loop(0, shards, shard_step, 0)

    returned_pages = returned.shape[1] // page_tokens
    first = ((me_ref[0] // 2) % 2) * (own_pages - returned_pages)

    def return_step(shard, carry):
        for page in range(returned_pages):
            start = pl.multiple_of(place[shard * own_pages + first + page], page_tokens)
            span = slice(page * page_tokens, (page + 1) * page_tokens)
            returned[shard, span] = ordered[pl.ds(start, page_tokens), :]
        return carry

    lax.fori_loop(0, shards, return_step, 0)


def blend(me, source, place, select, received):
    shards, wide, _ = received.shape
    tokens = select.shape[1]
    own_pages = source.shape[0] // shards
    page_tokens = tokens // own_pages
    returned_pages = (own_pages + 1) // 2
    smem = pl.BlockSpec(memory_space=SMEM)
    vmem = pl.BlockSpec(memory_space=VMEM)
    return pl.pallas_call(
        blend_kernel,
        in_specs=[smem, smem, smem, vmem, vmem],
        out_specs=[vmem, vmem],
        out_shape=[
            jax.ShapeDtypeStruct((shards * tokens, HEAD), BF16),
            jax.ShapeDtypeStruct((shards, returned_pages * page_tokens, HEAD), BF16),
        ],
        compiler_params=params(32),
        cost_estimate=pl.CostEstimate(flops=400000000, bytes_accessed=7000000, transcendentals=0),
        name="blend",
    )(me, source, place, select, received)


TILES = 8
CHUNK = 512


def attend_kernel(
    me_ref,
    tiles,
    tile_count,
    positions,
    queries,
    mine,
    other,
    out,
    keys,
    values,
    scores,
    block,
    block_position,
    sems,
):
    length = keys.shape[0]
    rows = queries.shape[1] // 2
    shards = queries.shape[0]
    per_shard = rows // 16
    tokens = length // shards
    half = TILES * 16
    core = me_ref[0] % 2

    @pl.when(core == 0)
    def _():
        pltpu.make_async_copy(mine, keys, sems.at[0]).start()
        pltpu.make_async_copy(other, values, sems.at[1]).start()

    @pl.when(core != 0)
    def _():
        pltpu.make_async_copy(other, keys, sems.at[0]).start()
        pltpu.make_async_copy(mine, values, sems.at[1]).start()

    out[...] = jnp.zeros_like(out)
    pltpu.make_async_copy(mine, keys, sems.at[0]).wait()
    pltpu.make_async_copy(mine, values, sems.at[1]).wait()

    def block_step(b, carry):
        first_tile = b * TILES
        for t in range(TILES):
            tile = tiles[first_tile + t]
            shard = tile // per_shard
            row = pl.multiple_of((tile - shard * per_shard) * 16, 16)
            low = slice(t * 16, (t + 1) * 16)
            high = slice(half + t * 16, half + (t + 1) * 16)
            block[low] = queries[shard, pl.ds(row, 16), :]
            block[high] = queries[shard, pl.ds(rows + row, 16), :]
            position = positions[pl.ds(pl.multiple_of(tile * 16, 16), 16), :]
            block_position[low] = position
            block_position[high] = position
        open_keys = (tiles[first_tile] // per_shard) * tokens
        seen_keys = (tiles[first_tile + TILES - 1] // per_shard + 1) * tokens
        open_chunks = open_keys // CHUNK
        seen_chunks = (seen_keys + CHUNK - 1) // CHUNK
        query = block[...]

        def score(chunk):
            start = pl.multiple_of(chunk * CHUNK, CHUNK)
            products = lax.dot_general(
                query,
                keys[pl.ds(start, CHUNK), :],
                (((1,), (1,)), ((), ())),
                preferred_element_type=F32,
            )
            return products * EXP2_SCALE

        def keep(chunk, found, best):
            scores[chunk] = found
            for lane in range(CHUNK // HEAD):
                best = jnp.maximum(best, found[:, lane * HEAD : (lane + 1) * HEAD])
            return best

        def open_step(chunk, best):
            return keep(chunk, score(chunk), best)

        def edge_step(chunk, best):
            found = score(chunk)
            key_position = chunk * CHUNK + lax.broadcasted_iota(I32, (2 * half, CHUNK), 1)
            row_position = jnp.concatenate([block_position[...]] * (CHUNK // HEAD), axis=1)
            return keep(chunk, jnp.where(key_position <= row_position, found, MASKED), best)

        best = jnp.full((2 * half, HEAD), MASKED, F32)
        best = lax.fori_loop(0, open_chunks, open_step, best)
        best = lax.fori_loop(open_chunks, seen_chunks, edge_step, best)
        row_best = jnp.max(best, axis=1, keepdims=True)

        def weigh(chunk, state):
            total, mixed = state
            start = pl.multiple_of(chunk * CHUNK, CHUNK)
            exps = jnp.exp2(scores[chunk] - row_best)
            for lane in range(CHUNK // HEAD):
                total = total + exps[:, lane * HEAD : (lane + 1) * HEAD]
            mixed = mixed + jnp.dot(
                exps.astype(BF16), values[pl.ds(start, CHUNK), :], preferred_element_type=F32
            )
            return total, mixed

        zero = jnp.zeros((2 * half, HEAD), F32)
        total, mixed = lax.fori_loop(0, seen_chunks, weigh, (zero, zero))
        total = jnp.sum(total, axis=1, keepdims=True)
        result = mixed / jnp.where(total > 0, total, 1.0)
        result = jnp.where(block_position[...] >= 0, result, 0.0).astype(BF16)
        for t in range(TILES):
            tile = tiles[first_tile + t]
            shard = tile // per_shard
            row = pl.multiple_of((tile - shard * per_shard) * 16, 16)
            out[shard, pl.ds(row, 16), :] = result[t * 16 : (t + 1) * 16]
            out[shard, pl.ds(rows + row, 16), :] = result[half + t * 16 : half + (t + 1) * 16]
        return carry

    lax.fori_loop(0, (tile_count[0] + TILES - 1) // TILES, block_step, 0)


def attend(me, tiles, tile_count, positions, queries, mine, other):
    length = mine.shape[0]
    smem = pl.BlockSpec(memory_space=SMEM)
    vmem = pl.BlockSpec(memory_space=VMEM)
    anywhere = pl.BlockSpec(memory_space=pl.ANY)
    block = 2 * TILES * 16
    return pl.pallas_call(
        attend_kernel,
        in_specs=[smem, smem, smem, vmem, vmem, anywhere, anywhere],
        out_specs=vmem,
        out_shape=jax.ShapeDtypeStruct(queries.shape, BF16),
        scratch_shapes=[
            pltpu.VMEM((length, HEAD), BF16),
            pltpu.VMEM((length, HEAD), BF16),
            pltpu.VMEM((length // CHUNK, block, CHUNK), F32),
            pltpu.VMEM((block, HEAD), BF16),
            pltpu.VMEM((block, HEAD), I32),
            pltpu.SemaphoreType.DMA((2,)),
        ],
        compiler_params=params(40),
        cost_estimate=pl.CostEstimate(
            flops=3000000000, bytes_accessed=5000000, transcendentals=6000000
        ),
        name="attend",
    )(me, tiles, tile_count, positions, queries, mine, other)


def place_cache_kernel(received, keys, values):
    own_pages, page_tokens, _ = keys.shape
    shared = received.shape[1] // page_tokens
    for part, target in ((0, keys), (1, values)):
        for page in range(own_pages):
            source, at = (part, page) if page < shared else (2 + part, page - own_pages + shared)
            target[page] = received[source, at * page_tokens : (at + 1) * page_tokens]


def place_cache(received, own_pages, page_tokens):
    shards, sent, _ = received.shape
    group = shards // KV_HEADS
    cache = jax.ShapeDtypeStruct((own_pages, page_tokens, KV_HEADS * HEAD), BF16)
    spec = pl.BlockSpec((own_pages, page_tokens, HEAD), lambda h: (0, 0, h))
    return pl.pallas_call(
        place_cache_kernel,
        grid=(KV_HEADS,),
        in_specs=[pl.BlockSpec((group, sent, HEAD), lambda h: (h, 0, 0))],
        out_specs=[spec, spec],
        out_shape=[cache, cache],
        compiler_params=params(24),
        cost_estimate=pl.CostEstimate(flops=0, bytes_accessed=1500000, transcendentals=0),
        name="place_cache",
    )(received)


def place_attended_kernel(received, out):
    rows = out.shape[0]
    for j in range(received.shape[0]):
        for t in range(2):
            head = 2 * j + t
            out[:, head * HEAD : (head + 1) * HEAD] = received[j, t * rows : (t + 1) * rows]


def place_attended(received):
    shards, sent, _ = received.shape
    steps = 4
    rows, width = sent // 2, shards * 2 * HEAD
    return pl.pallas_call(
        place_attended_kernel,
        grid=(steps,),
        in_specs=[pl.BlockSpec((shards // steps, sent, HEAD), lambda h: (h, 0, 0))],
        out_specs=pl.BlockSpec((rows, width // steps), lambda h: (0, h)),
        out_shape=jax.ShapeDtypeStruct((rows, width), BF16),
        compiler_params=params(24),
        cost_estimate=pl.CostEstimate(flops=0, bytes_accessed=1600000, transcendentals=0),
        name="place_attended",
    )(received)


def exchange(blocks):
    return lax.all_to_all(blocks, "shard", 0, 0)


def shard_program(
    shards,
    paged_key_store,
    paged_value_store,
    paged_scale_store,
    page_map,
    span_order,
    listed_count,
    listed_index,
    listed_queries,
    selected_token_keys,
    selected_token_values,
):
    own_pages, page_tokens, _ = paged_key_store.shape
    rows = listed_queries.shape[0]
    tokens = own_pages * page_tokens
    me = lax.axis_index("shard").astype(I32).reshape(1)

    sent_kv, cosine, sine = prepare_kv(
        me,
        page_map,
        span_order,
        listed_index,
        paged_scale_store,
        paged_key_store,
        paged_value_store,
        selected_token_keys,
        selected_token_values,
        shards,
    )
    received_kv = exchange(sent_kv)
    received_queries = exchange(prepare_queries(listed_queries, cosine, sine, shards))

    listed = jnp.arange(rows, dtype=I32)[None, :] < listed_count[:, None]
    listed_lanes = jnp.where(listed, listed_index.reshape(shards, rows), -1)
    listed_lanes = jnp.pad(listed_lanes, ((0, 0), (tokens, 0)), constant_values=-1)
    source, place, tiles, tile_count, positions, select = plan(
        page_map, span_order, listed_count, listed_lanes, tokens
    )

    mine, returned = blend(me, source, place, select, received_kv)
    other = lax.ppermute(mine, "shard", [(i, i ^ 1) for i in range(shards)])
    received_cache = exchange(returned)
    attended = attend(me, tiles, tile_count, positions, received_queries, mine, other)
    mixed_keys, mixed_values = place_cache(received_cache, own_pages, page_tokens)
    return mixed_keys, mixed_values, place_attended(exchange(attended))


def solution(mesh):
    split = ("req", "shard")
    in_specs = (
        P(split, None, None),
        P(split, None, None),
        P(split, None, None),
        P("req"),
        P("req"),
        P("req"),
        P("req"),
        P(split, None),
        P(split, None),
        P(split, None),
    )
    out_specs = (P(split, None, None), P(split, None, None), P(split, None))
    return jax.shard_map(
        functools.partial(shard_program, mesh.shape["shard"]),
        mesh=mesh,
        in_specs=in_specs,
        out_specs=out_specs,
        check_vma=False,
    )
```

```python
import functools

import jax
import jax.numpy as jnp
import numpy as np
from jax import lax
from jax.experimental import pallas as pl
from jax.experimental.pallas import tpu as pltpu
from jax.sharding import PartitionSpec as P

HEAD = 128
KV_HEADS = 8
SPAN_LEN = 704
ROPE_BASE = 1000000.0
MASKED = -1e30
VMEM_MIB = 56
TILES = 16
CHUNK = 1408
TURN = 512
PAGE = 16
EXP2_SCALE = float(HEAD**-0.5 / np.log(2.0))

BF16 = jnp.bfloat16
F32 = jnp.float32
I32 = jnp.int32
SMEM = pltpu.SMEM
VMEM = pltpu.VMEM


def rope_frequency():
    half = HEAD // 2
    frequency = ROPE_BASE ** (-(np.arange(half, dtype=np.float64) * 2.0) / HEAD)
    return np.concatenate([frequency, frequency]).astype(np.float32)[None, :]


def rope_tables(position, frequency):
    angles = position * frequency
    lane = lax.broadcasted_iota(I32, angles.shape, 1)
    sine = jnp.sin(angles)
    return jnp.cos(angles), jnp.where(lane < HEAD // 2, -sine, sine)


def rotate(x, cosine, sine):
    return x * cosine + pltpu.roll(x, HEAD // 2, 1) * sine


def params(mib, **more):
    return pltpu.CompilerParams(vmem_limit_bytes=mib * 1024 * 1024, **more)


def prepare_kernel(
    me_ref,
    page_map,
    span_order,
    listed_index,
    scale,
    frequency,
    queries,
    keys,
    values,
    fresh_keys,
    fresh_values,
    out,
    slots,
    positions,
    row_cos,
    row_sin,
    shift_cos,
    shift_sin,
):
    head = pl.program_id(0)
    me = me_ref[0]
    own_pages, page_tokens, _ = keys.shape
    rows = fresh_keys.shape[0]
    group = out.shape[0]
    span_count = span_order.shape[0]
    per_span = page_map.shape[0] // span_count
    tokens = own_pages * page_tokens

    @pl.when(head == 0)
    def _():
        first = me * own_pages
        for slot in range(span_count):
            start = span_order[slot] * per_span

            def note(p, carry):
                place = page_map[start + p] - first
                inside = (place >= 0) & (place < own_pages)
                slots[jnp.where(inside, place, own_pages)] = slot
                return carry

            lax.fori_loop(0, per_span, note, 0, unroll=11)
        for c in range(rows):
            position = (me * tokens + listed_index[me * rows + c]).astype(F32)
            positions[c : c + 1, :] = jnp.full((1, HEAD), position, F32)
        row_cos[...], row_sin[...] = rope_tables(positions[...], frequency[...])
        shift = lax.broadcasted_iota(I32, (span_count, HEAD), 0) * SPAN_LEN
        shift_cos[...], shift_sin[...] = rope_tables(shift.astype(F32), frequency[...])

    cosine, sine = row_cos[...], row_sin[...]
    for j in range(group):
        for t in range(2):
            at = (2 * j + t) * HEAD
            x = queries[:, at : at + HEAD].astype(F32)
            out[j, t * rows : (t + 1) * rows] = rotate(x, cosine, sine).astype(BF16)
    base = 2 * rows
    for page in range(own_pages):
        slot = slots[page]
        page_cos = shift_cos[pl.ds(slot, 1), :]
        page_sin = shift_sin[pl.ds(slot, 1), :]
        span = slice(base + page * page_tokens, base + (page + 1) * page_tokens)
        key = keys[page].astype(F32) * scale[0, head, page]
        key = rotate(key, page_cos, page_sin).astype(BF16)
        value = (values[page].astype(F32) * scale[1, head, page]).astype(BF16)
        for j in range(group):
            out[j, span] = value if j % 2 else key
    key = rotate(fresh_keys[...].astype(F32), cosine, sine).astype(BF16)
    value = fresh_values[...]
    for j in range(group):
        out[j, base + tokens :] = value if j % 2 else key


def prepare(
    me,
    page_map,
    span_order,
    listed_index,
    scale,
    queries,
    keys,
    values,
    fresh_keys,
    fresh_values,
    shards,
):
    own_pages, page_tokens, _ = keys.shape
    rows, width = queries.shape
    sent = 3 * rows + own_pages * page_tokens
    smem = pl.BlockSpec(memory_space=SMEM)
    pages = pl.BlockSpec((own_pages, page_tokens, HEAD), lambda h: (0, 0, h))
    fresh = pl.BlockSpec((rows, HEAD), lambda h: (0, h))
    return pl.pallas_call(
        prepare_kernel,
        grid=(KV_HEADS,),
        in_specs=[
            smem,
            smem,
            smem,
            smem,
            smem,
            pl.BlockSpec((1, HEAD), lambda h: (0, 0)),
            pl.BlockSpec((rows, width // KV_HEADS), lambda h: (0, h)),
            pages,
            pages,
            fresh,
            fresh,
        ],
        out_specs=pl.BlockSpec((shards // KV_HEADS, sent, HEAD), lambda h: (h, 0, 0)),
        out_shape=jax.ShapeDtypeStruct((shards, sent, HEAD), BF16),
        scratch_shapes=[
            pltpu.SMEM((own_pages + 1,), I32),
            pltpu.VMEM((rows, HEAD), F32),
            pltpu.VMEM((rows, HEAD), F32),
            pltpu.VMEM((rows, HEAD), F32),
            pltpu.VMEM((span_order.shape[0], HEAD), F32),
            pltpu.VMEM((span_order.shape[0], HEAD), F32),
        ],
        compiler_params=params(VMEM_MIB),
        cost_estimate=pl.CostEstimate(
            flops=5000000000, bytes_accessed=4300000, transcendentals=0
        ),
        name="prepare",
    )(
        me,
        page_map,
        span_order,
        listed_index,
        scale,
        jnp.asarray(rope_frequency()),
        queries,
        keys,
        values,
        fresh_keys,
        fresh_values,
    )


def plan_kernel(
    page_map,
    span_order,
    listed_count,
    listed_lanes,
    source,
    place,
    tiles,
    block_count,
    positions,
    row_position,
):
    shards, rows = listed_lanes.shape
    pages = page_map.shape[0]
    own_pages = pages // shards
    page_tokens = PAGE
    tokens = own_pages * page_tokens
    sent = tokens + 3 * rows
    span_count = span_order.shape[0]
    per_span = pages // span_count

    for slot in range(span_count):
        start = span_order[slot] * per_span

        def note(p, carry):
            stored = page_map[start + p]
            logical = slot * per_span + p
            owner = stored // own_pages
            within = stored - owner * own_pages
            source[logical] = owner * sent + 2 * rows + within * page_tokens
            place[stored] = logical * page_tokens
            return carry

        lax.fori_loop(0, per_span, note, 0, unroll=4)

    def count_tiles(shard, total):
        return total + (listed_count[shard] + 15) // 16

    total = lax.fori_loop(0, shards, count_tiles, 0)
    blocks = (total + TILES - 1) // TILES
    block_count[0] = blocks
    for k in range(TILES):
        tiles[k] = 0

    def list_tiles(shard, filled):
        count = listed_count[shard]
        for k in range(rows // 16):
            tiles[filled] = shard * (rows // 16) + k
            filled = filled + jnp.where(count > 16 * k, 1, 0)
        return filled

    lax.fori_loop(0, shards, list_tiles, blocks * TILES - total)

    diagonal = lax.broadcasted_iota(I32, (rows, rows), 0) == lax.broadcasted_iota(
        I32, (rows, rows), 1
    )

    def fill(shard, carry):
        listed = listed_lanes[pl.ds(shard, 1), :].astype(F32)
        offset = jnp.sum(jnp.where(diagonal, listed, 0.0), axis=1, keepdims=True)
        position = jnp.where(offset < 0.0, -1.0, offset + (shard * tokens).astype(F32))
        start = pl.multiple_of(shard * rows, 16)
        row_position[pl.ds(start, rows), :] = jnp.broadcast_to(position, (rows, HEAD))
        return carry

    lax.fori_loop(0, shards, fill, 0)

    def place_positions(b, carry):
        lanes = []
        for t in range(0, TILES, 8):
            found = []
            for u in range(t, t + 8):
                start = pl.multiple_of(tiles[b * TILES + u] * 16, 16)
                found.append(row_position[pl.ds(start, 16), :])
            lanes.append(jnp.concatenate(found, axis=0).T[:8])
        positions[b] = jnp.concatenate(lanes + lanes, axis=1).astype(I32)
        return carry

    lax.fori_loop(0, blocks, place_positions, 0)


def plan(page_map, span_order, listed_count, listed_lanes):
    shards, rows = listed_lanes.shape
    smem = pl.BlockSpec(memory_space=SMEM)
    vmem = pl.BlockSpec(memory_space=VMEM)
    pages = page_map.shape[0]
    block_limit = pl.cdiv(shards * (rows // 16), TILES)
    return pl.pallas_call(
        plan_kernel,
        in_specs=[smem, smem, smem, vmem],
        out_specs=[smem, smem, smem, smem, vmem],
        out_shape=[
            jax.ShapeDtypeStruct((pages,), I32),
            jax.ShapeDtypeStruct((pages,), I32),
            jax.ShapeDtypeStruct(((block_limit + 1) * TILES,), I32),
            jax.ShapeDtypeStruct((1,), I32),
            jax.ShapeDtypeStruct((block_limit, 8, 32 * TILES), I32),
        ],
        scratch_shapes=[pltpu.VMEM((shards * rows, HEAD), F32)],
        compiler_params=params(16),
        cost_estimate=pl.CostEstimate(
            flops=9000000000, bytes_accessed=3000000, transcendentals=0
        ),
        name="plan",
    )(page_map, span_order, listed_count, listed_lanes)


def blend_kernel(me_ref, source, place, listed_lanes, received, ordered, returned):
    shards, sent, _ = received.shape
    rows = listed_lanes.shape[1]
    own_pages = source.shape[0] // shards
    page_tokens = PAGE
    tokens = own_pages * page_tokens
    flat = received.reshape(shards * sent, HEAD)
    token = lax.broadcasted_iota(I32, (tokens, rows), 0)
    ones = jnp.ones((rows, HEAD), BF16)

    def shard_step(shard, carry):
        pages = []
        for page in range(own_pages):
            start = pl.multiple_of(source[shard * own_pages + page], page_tokens)
            pages.append(flat[pl.ds(start, page_tokens), :])
        cached = jnp.concatenate(pages, axis=0)
        pick = jnp.where(listed_lanes[pl.ds(shard, 1), :] == token, 1.0, 0.0).astype(BF16)
        fresh = jnp.concatenate([received[shard, 2 * rows + tokens :, :], ones], axis=1)
        found = jnp.dot(pick, fresh, preferred_element_type=F32)
        mixed = jnp.where(found[:, HEAD:] > 0.5, found[:, :HEAD], cached.astype(F32))
        start = pl.multiple_of(shard * tokens, 16)
        ordered[pl.ds(start, tokens), :] = mixed.astype(BF16)
        return carry

    lax.fori_loop(0, shards, shard_step, 0, unroll=4)

    returned_pages = returned.shape[1] // page_tokens
    first = ((me_ref[0] // 2) % 2) * (own_pages - returned_pages)

    def return_step(shard, carry):
        for page in range(returned_pages):
            start = pl.multiple_of(place[shard * own_pages + first + page], page_tokens)
            span = slice(page * page_tokens, (page + 1) * page_tokens)
            returned[shard, span] = ordered[pl.ds(start, page_tokens), :]
        return carry

    lax.fori_loop(0, shards, return_step, 0, unroll=4)


def blend(me, source, place, listed_lanes, received):
    shards, rows = listed_lanes.shape
    own_pages = source.shape[0] // shards
    returned_pages = (own_pages + 1) // 2
    smem = pl.BlockSpec(memory_space=SMEM)
    vmem = pl.BlockSpec(memory_space=VMEM)
    return pl.pallas_call(
        blend_kernel,
        in_specs=[smem, smem, smem, vmem, vmem],
        out_specs=[vmem, vmem],
        out_shape=[
            jax.ShapeDtypeStruct((source.shape[0] * PAGE, HEAD), BF16),
            jax.ShapeDtypeStruct((shards, returned_pages * PAGE, HEAD), BF16),
        ],
        compiler_params=params(16),
        cost_estimate=pl.CostEstimate(
            flops=4000000000, bytes_accessed=3000000, transcendentals=0
        ),
        name="blend",
    )(me, source, place, listed_lanes, received)


def turn_kernel(me_ref, mine, other, keys, values_t, longest, values, sems):
    length = keys.shape[0]
    core = me_ref[0] % 2

    @pl.when(core == 0)
    def _():
        pltpu.make_async_copy(mine, keys, sems.at[0]).start()
        pltpu.make_async_copy(other, values, sems.at[1]).start()

    @pl.when(core != 0)
    def _():
        pltpu.make_async_copy(other, keys, sems.at[0]).start()
        pltpu.make_async_copy(mine, values, sems.at[1]).start()

    pltpu.make_async_copy(mine, keys, sems.at[0]).wait()
    pltpu.make_async_copy(mine, values, sems.at[1]).wait()
    values_t[HEAD:, :] = jnp.ones((values_t.shape[0] - HEAD, length), BF16)
    ones = jnp.ones((HEAD, HEAD), BF16)
    most = jnp.zeros((8, HEAD), F32)
    for part in range(length // TURN):
        span = slice(part * TURN, (part + 1) * TURN)
        values_t[:HEAD, span] = values[span].T
        key = keys[span].astype(F32)
        squares = jnp.dot((key * key).astype(BF16), ones, preferred_element_type=F32)
        most = jnp.maximum(most, jnp.max(squares.reshape(TURN // 8, 8, HEAD), axis=0))
    longest[...] = jnp.broadcast_to(jnp.max(most, axis=0, keepdims=True), (8, HEAD))


def turn(me, mine, other):
    length = mine.shape[0]
    vmem = pl.BlockSpec(memory_space=VMEM)
    anywhere = pl.BlockSpec(memory_space=pl.ANY)
    return pl.pallas_call(
        turn_kernel,
        in_specs=[pl.BlockSpec(memory_space=SMEM), anywhere, anywhere],
        out_specs=[vmem, vmem, vmem],
        out_shape=[
            jax.ShapeDtypeStruct((length, HEAD), BF16),
            jax.ShapeDtypeStruct((HEAD + 16, length), BF16),
            jax.ShapeDtypeStruct((8, HEAD), F32),
        ],
        scratch_shapes=[pltpu.VMEM((length, HEAD), BF16), pltpu.SemaphoreType.DMA((2,))],
        compiler_params=params(16),
        cost_estimate=pl.CostEstimate(
            flops=100000000, bytes_accessed=3000000, transcendentals=0
        ),
        name="turn",
    )(me, mine, other)


SLACK = 60.0
LEAST = 2.0**-90


def attend_kernel(
    tiles, block_count, positions, longest, received, keys, values_t, out, scores, block
):
    length = keys.shape[0]
    shards = out.shape[0]
    rows = out.shape[1] // 2
    per_shard = rows // 16
    tokens = length // shards
    half = TILES * 16
    wide = 2 * half
    out[...] = jnp.zeros_like(out)

    def block_step(b, carry):
        first_tile = b * TILES
        for t in range(TILES):
            tile = tiles[first_tile + t]
            shard = tile // per_shard
            row = pl.multiple_of((tile - shard * per_shard) * 16, 16)
            block[t * 16 : (t + 1) * 16] = received[shard, pl.ds(row, 16), :]
            block[half + t * 16 : half + (t + 1) * 16] = received[shard, pl.ds(rows + row, 16), :]
        open_keys = (tiles[first_tile] // per_shard) * tokens
        seen_keys = (tiles[first_tile + TILES - 1] // per_shard + 1) * tokens
        open_chunks = open_keys // CHUNK
        seen_chunks = (seen_keys + CHUNK - 1) // CHUNK
        query = block[...]
        position = positions[b][:1]

        def score(chunk):
            start = pl.multiple_of(chunk * CHUNK, CHUNK)
            products = lax.dot_general(
                keys[pl.ds(start, CHUNK), :],
                query,
                (((1,), (1,)), ((), ())),
                preferred_element_type=F32,
            )
            return products * EXP2_SCALE

        def edge_score(chunk):
            found = score(chunk)
            key_position = chunk * CHUNK + lax.broadcasted_iota(I32, (CHUNK, wide), 0)
            return jnp.where(key_position <= position, found, MASKED)

        def add(chunk, found, shift, state):
            start = pl.multiple_of(chunk * CHUNK, CHUNK)
            exps = jnp.exp2(found - shift).astype(BF16)
            return state + jnp.dot(
                values_t[:, pl.ds(start, CHUNK)], exps, preferred_element_type=F32
            )

        def finish(state):
            total = state[HEAD : HEAD + 1]
            result = state[:HEAD] / jnp.where(total > 0, total, 1.0)
            result = jnp.where(position >= 0, result, 0.0).T.astype(BF16)
            for t in range(TILES):
                tile = tiles[first_tile + t]
                shard = tile // per_shard
                row = pl.multiple_of((tile - shard * per_shard) * 16, 16)
                out[shard, pl.ds(row, 16), :] = result[t * 16 : (t + 1) * 16]
                out[shard, pl.ds(rows + row, 16), :] = result[half + t * 16 : half + (t + 1) * 16]
            return total

        nothing = jnp.zeros((values_t.shape[0], wide), F32)
        squares = query.astype(F32)
        squares = lax.dot_general(
            jnp.ones((8, HEAD), BF16),
            (squares * squares).astype(BF16),
            (((1,), (1,)), ((), ())),
            preferred_element_type=F32,
        )
        bound = jnp.sqrt(squares[:1] * longest[:1, :1]) * (1.02 * EXP2_SCALE) - SLACK
        state = lax.fori_loop(
            0, open_chunks, lambda c, st: add(c, score(c), bound, st), nothing
        )
        state = lax.fori_loop(
            open_chunks, seen_chunks, lambda c, st: add(c, edge_score(c), bound, st), state
        )
        total = finish(state)
        lowest = jnp.min(jnp.where(position >= 0, total, 1.0))

        @pl.when(lowest < LEAST)
        def _():
            def keep(chunk, best):
                found = edge_score(chunk)
                scores[chunk] = found
                return jnp.maximum(best, jnp.max(found.reshape(CHUNK // 8, 8, wide), axis=0))

            best = lax.fori_loop(0, seen_chunks, keep, jnp.full((8, wide), MASKED, F32))
            best = jnp.max(best, axis=0, keepdims=True)
            finish(
                lax.fori_loop(
                    0, seen_chunks, lambda c, st: add(c, scores[c], best, st), nothing
                )
            )

        return carry

    lax.fori_loop(0, block_count[0], block_step, 0)


def attend(tiles, block_count, positions, longest, received, keys, values_t, rows):
    length = keys.shape[0]
    smem = pl.BlockSpec(memory_space=SMEM)
    vmem = pl.BlockSpec(memory_space=VMEM)
    block = 2 * TILES * 16
    return pl.pallas_call(
        attend_kernel,
        in_specs=[smem, smem, vmem, vmem, vmem, vmem, vmem],
        out_specs=vmem,
        out_shape=jax.ShapeDtypeStruct((received.shape[0], 2 * rows, HEAD), BF16),
        scratch_shapes=[
            pltpu.VMEM((length // CHUNK, CHUNK, block), F32),
            pltpu.VMEM((block, HEAD), BF16),
        ],
        compiler_params=params(28),
        cost_estimate=pl.CostEstimate(
            flops=16000000000, bytes_accessed=3000000, transcendentals=0
        ),
        name="attend",
    )(tiles, block_count, positions, longest, received, keys, values_t)


def place_cache_kernel(received, keys, values):
    own_pages, page_tokens, _ = keys.shape
    shared = received.shape[1] // page_tokens
    for part, target in ((0, keys), (1, values)):
        for page in range(own_pages):
            source, at = (part, page) if page < shared else (2 + part, page - own_pages + shared)
            target[page] = received[source, at * page_tokens : (at + 1) * page_tokens]


def place_cache(received, own_pages, page_tokens):
    shards, sent, _ = received.shape
    group = shards // KV_HEADS
    cache = jax.ShapeDtypeStruct((own_pages, page_tokens, KV_HEADS * HEAD), BF16)
    spec = pl.BlockSpec((own_pages, page_tokens, HEAD), lambda h: (0, 0, h))
    return pl.pallas_call(
        place_cache_kernel,
        grid=(KV_HEADS,),
        in_specs=[pl.BlockSpec((group, sent, HEAD), lambda h: (h, 0, 0))],
        out_specs=[spec, spec],
        out_shape=[cache, cache],
        compiler_params=params(16),
        cost_estimate=pl.CostEstimate(
            flops=2500000000, bytes_accessed=3000000, transcendentals=0
        ),
        name="place_cache",
    )(received)


def place_attended_kernel(received, out):
    rows = out.shape[0]
    for j in range(received.shape[0]):
        for t in range(2):
            head = 2 * j + t
            out[:, head * HEAD : (head + 1) * HEAD] = received[j, t * rows : (t + 1) * rows]


def place_attended(received):
    shards, sent, _ = received.shape
    steps = 4
    rows, width = sent // 2, shards * 2 * HEAD
    return pl.pallas_call(
        place_attended_kernel,
        grid=(steps,),
        in_specs=[pl.BlockSpec((shards // steps, sent, HEAD), lambda h: (h, 0, 0))],
        out_specs=pl.BlockSpec((rows, width // steps), lambda h: (0, h)),
        out_shape=jax.ShapeDtypeStruct((rows, width), BF16),
        compiler_params=params(16),
        cost_estimate=pl.CostEstimate(flops=0, bytes_accessed=1600000, transcendentals=0),
        name="place_attended",
    )(received)


def exchange(blocks):
    return lax.all_to_all(blocks, "shard", 0, 0)


def shard_program(
    shards,
    paged_key_store,
    paged_value_store,
    paged_scale_store,
    page_map,
    span_order,
    listed_count,
    listed_index,
    listed_queries,
    selected_token_keys,
    selected_token_values,
):
    own_pages, page_tokens, _ = paged_key_store.shape
    rows = listed_queries.shape[0]
    me = lax.axis_index("shard").astype(I32).reshape(1)

    received = exchange(
        prepare(
            me,
            page_map,
            span_order,
            listed_index,
            paged_scale_store.transpose(1, 2, 0),
            listed_queries,
            paged_key_store,
            paged_value_store,
            selected_token_keys,
            selected_token_values,
            shards,
        )
    )

    listed = jnp.arange(rows, dtype=I32)[None, :] < listed_count[:, None]
    listed_lanes = jnp.where(listed, listed_index.reshape(shards, rows), -1)
    source, place, tiles, block_count, positions = plan(
        page_map, span_order, listed_count, listed_lanes
    )

    mine, returned = blend(me, source, place, listed_lanes, received)
    other = lax.ppermute(mine, "shard", [(i, i ^ 1) for i in range(shards)])
    received_cache = exchange(returned)
    keys, values_t, longest = turn(me, mine, other)
    attended = attend(tiles, block_count, positions, longest, received, keys, values_t, rows)
    mixed_keys, mixed_values = place_cache(received_cache, own_pages, page_tokens)
    return mixed_keys, mixed_values, place_attended(exchange(attended))


def solution(mesh):
    split = ("req", "shard")
    in_specs = (
        P(split, None, None),
        P(split, None, None),
        P(split, None, None),
        P("req"),
        P("req"),
        P("req"),
        P("req"),
        P(split, None),
        P(split, None),
        P(split, None),
    )
    out_specs = (P(split, None, None), P(split, None, None), P(split, None))
    return jax.shard_map(
        functools.partial(shard_program, mesh.shape["shard"]),
        mesh=mesh,
        in_specs=in_specs,
        out_specs=out_specs,
        check_vma=False,
    )
```

```python
import functools

import jax
import jax.numpy as jnp
import numpy as np
from jax import lax
from jax.experimental import pallas as pl
from jax.experimental.pallas import tpu as pltpu
from jax.sharding import PartitionSpec as P

HEAD = 128
KV_HEADS = 8
SPAN_LEN = 704
ROPE_BASE = 1000000.0
MASKED = -1e30
VMEM_MIB = 56
TILES = 16
CHUNK = 1408
PAGE = 16
BIG = 22
MID = 11
SMALL = 4
EXP2_SCALE = float(HEAD**-0.5 / np.log(2.0))

BF16 = jnp.bfloat16
F32 = jnp.float32
I32 = jnp.int32
SMEM = pltpu.SMEM
VMEM = pltpu.VMEM
OUT_SPACE = pltpu.HBM


def rope_frequency():
    half = HEAD // 2
    frequency = ROPE_BASE ** (-(np.arange(half, dtype=np.float64) * 2.0) / HEAD)
    return np.concatenate([frequency, frequency]).astype(np.float32)[None, :]


def rope_tables(position, frequency):
    angles = position * frequency
    lane = lax.broadcasted_iota(I32, angles.shape, 1)
    sine = jnp.sin(angles)
    return jnp.cos(angles), jnp.where(lane < HEAD // 2, -sine, sine)


def rotate(x, cosine, sine):
    return x * cosine + pltpu.roll(x, HEAD // 2, 1) * sine


def params(mib, **more):
    return pltpu.CompilerParams(vmem_limit_bytes=mib * 1024 * 1024, **more)


def prepare_kernel(
    me_ref,
    page_map,
    span_order,
    listed_index,
    scale,
    frequency,
    queries_in,
    keys_in,
    values_in,
    fresh_keys_in,
    fresh_values_in,
    out,
    queries,
    keys,
    values,
    fresh_keys,
    fresh_values,
    blocks,
    slots,
    positions,
    shift_cos,
    shift_sin,
    in_sems,
    out_sems,
):
    me = me_ref[0]
    own_pages, page_tokens, _ = keys.shape
    rows = fresh_keys.shape[0]
    group = blocks.shape[0] // KV_HEADS
    span_count = span_order.shape[0]
    per_span = page_map.shape[0] // span_count
    tokens = own_pages * page_tokens
    arrivals = [
        pltpu.make_async_copy(source, target, in_sems.at[i])
        for i, (source, target) in enumerate(
            (
                (queries_in, queries),
                (keys_in, keys),
                (values_in, values),
                (fresh_keys_in, fresh_keys),
                (fresh_values_in, fresh_values),
            )
        )
    ]
    for arrival in arrivals:
        arrival.start()

    for c in range(rows):
        position = (me * tokens + listed_index[me * rows + c]).astype(F32)
        positions[c : c + 1, :] = jnp.full((1, HEAD), position, F32)
    cosine, sine = rope_tables(positions[...], frequency[...])
    shift = lax.broadcasted_iota(I32, (span_count, HEAD), 0) * SPAN_LEN
    shift_cos[...], shift_sin[...] = rope_tables(shift.astype(F32), frequency[...])
    first = me * own_pages
    for slot in range(span_count):
        start = span_order[slot] * per_span

        def note(p, carry):
            place = page_map[start + p] - first
            inside = (place >= 0) & (place < own_pages)
            slots[jnp.where(inside, place, own_pages)] = slot
            return carry

        lax.fori_loop(0, per_span, note, 0, unroll=11)
    page_slots = [slots[page] for page in range(own_pages)]
    for arrival in arrivals:
        arrival.wait()

    departures = []
    for head in range(KV_HEADS):
        lanes = slice(head * HEAD, (head + 1) * HEAD)
        outs = [head * group + j for j in range(group)]
        for j in range(group):
            for t in range(2):
                at = (2 * (head * group + j) + t) * HEAD
                x = queries[:, at : at + HEAD].astype(F32)
                blocks[outs[j], t * rows : (t + 1) * rows] = rotate(x, cosine, sine).astype(BF16)
        base = 2 * rows
        for page in range(own_pages):
            page_cos = shift_cos[pl.ds(page_slots[page], 1), :]
            page_sin = shift_sin[pl.ds(page_slots[page], 1), :]
            span = slice(base + page * page_tokens, base + (page + 1) * page_tokens)
            key = keys[page, :, lanes].astype(F32) * scale[0, head, page]
            key = rotate(key, page_cos, page_sin).astype(BF16)
            value = (values[page, :, lanes].astype(F32) * scale[1, head, page]).astype(BF16)
            for j in range(group):
                blocks[outs[j], span] = value if j % 2 else key
        key = rotate(fresh_keys[:, lanes].astype(F32), cosine, sine).astype(BF16)
        value = fresh_values[:, lanes]
        for j in range(group):
            blocks[outs[j], base + tokens :] = value if j % 2 else key
        span = pl.ds(head * group, group)
        departures.append(
            pltpu.make_async_copy(blocks.at[span], out.at[span], out_sems.at[head])
        )
        departures[-1].start()
    for departure in departures:
        departure.wait()


def prepare(
    me,
    page_map,
    span_order,
    listed_index,
    scale,
    queries,
    keys,
    values,
    fresh_keys,
    fresh_values,
    shards,
):
    own_pages, page_tokens, _ = keys.shape
    rows, width = queries.shape
    sent = 3 * rows + own_pages * page_tokens
    smem = pl.BlockSpec(memory_space=SMEM)
    vmem = pl.BlockSpec(memory_space=VMEM)
    anywhere = pl.BlockSpec(memory_space=pl.ANY)
    arrays = (queries, keys, values, fresh_keys, fresh_values)
    return pl.pallas_call(
        prepare_kernel,
        in_specs=[smem] * 5 + [vmem] + [anywhere] * 5,
        out_specs=pl.BlockSpec(memory_space=OUT_SPACE),
        out_shape=jax.ShapeDtypeStruct((shards, sent, HEAD), BF16),
        scratch_shapes=[pltpu.VMEM(a.shape, a.dtype) for a in arrays]
        + [
            pltpu.VMEM((shards, sent, HEAD), BF16),
            pltpu.SMEM((own_pages + 1,), I32),
            pltpu.VMEM((rows, HEAD), F32),
            pltpu.VMEM((span_order.shape[0], HEAD), F32),
            pltpu.VMEM((span_order.shape[0], HEAD), F32),
            pltpu.SemaphoreType.DMA((len(arrays),)),
            pltpu.SemaphoreType.DMA((KV_HEADS,)),
        ],
        compiler_params=params(VMEM_MIB),
        cost_estimate=pl.CostEstimate(
            flops=5000000000, bytes_accessed=4300000, transcendentals=0
        ),
        name="prepare",
    )(
        me,
        page_map,
        span_order,
        listed_index,
        scale,
        jnp.asarray(rope_frequency()),
        *arrays,
    )


def plan_kernel(
    page_map,
    span_order,
    listed_count,
    listed_lanes,
    source,
    place,
    tiles,
    block_count,
    positions,
    row_position,
):
    shards, rows = listed_lanes.shape
    pages = page_map.shape[0]
    own_pages = pages // shards
    page_tokens = PAGE
    tokens = own_pages * page_tokens
    sent = tokens + 3 * rows
    span_count = span_order.shape[0]
    per_span = pages // span_count

    for slot in range(span_count):
        start = span_order[slot] * per_span

        def note(p, carry):
            stored = page_map[start + p]
            logical = slot * per_span + p
            owner = stored // own_pages
            within = stored - owner * own_pages
            source[logical] = owner * sent + 2 * rows + within * page_tokens
            place[stored] = logical * page_tokens
            return carry

        lax.fori_loop(0, per_span, note, 0, unroll=4)

    def count_tiles(shard, total):
        return total + (listed_count[shard] + 15) // 16

    total = lax.fori_loop(0, shards, count_tiles, 0)
    blocks = (total + TILES - 1) // TILES
    block_count[0] = blocks
    for k in range(TILES):
        tiles[k] = 0

    def list_tiles(shard, filled):
        count = listed_count[shard]
        for k in range(rows // 16):
            tiles[filled] = shard * (rows // 16) + k
            filled = filled + jnp.where(count > 16 * k, 1, 0)
        return filled

    lax.fori_loop(0, shards, list_tiles, blocks * TILES - total)

    diagonal = lax.broadcasted_iota(I32, (rows, rows), 0) == lax.broadcasted_iota(
        I32, (rows, rows), 1
    )

    def fill(shard, carry):
        listed = listed_lanes[pl.ds(shard, 1), :].astype(F32)
        offset = jnp.sum(jnp.where(diagonal, listed, 0.0), axis=1, keepdims=True)
        position = jnp.where(offset < 0.0, -1.0, offset + (shard * tokens).astype(F32))
        start = pl.multiple_of(shard * rows, 16)
        row_position[pl.ds(start, rows), :] = jnp.broadcast_to(position, (rows, HEAD))
        return carry

    lax.fori_loop(0, shards, fill, 0)

    def place_positions(b, carry):
        lanes = []
        for t in range(0, TILES, 8):
            found = []
            for u in range(t, t + 8):
                start = pl.multiple_of(tiles[b * TILES + u] * 16, 16)
                found.append(row_position[pl.ds(start, 16), :])
            lanes.append(jnp.concatenate(found, axis=0).T[:8])
        positions[b] = jnp.concatenate(lanes + lanes, axis=1).astype(I32)
        return carry

    lax.fori_loop(0, blocks, place_positions, 0)


def plan(page_map, span_order, listed_count, listed_lanes):
    shards, rows = listed_lanes.shape
    smem = pl.BlockSpec(memory_space=SMEM)
    vmem = pl.BlockSpec(memory_space=VMEM)
    pages = page_map.shape[0]
    block_limit = pl.cdiv(shards * (rows // 16), TILES)
    return pl.pallas_call(
        plan_kernel,
        in_specs=[smem, smem, smem, vmem],
        out_specs=[smem, smem, smem, smem, vmem],
        out_shape=[
            jax.ShapeDtypeStruct((pages,), I32),
            jax.ShapeDtypeStruct((pages,), I32),
            jax.ShapeDtypeStruct(((block_limit + 1) * TILES,), I32),
            jax.ShapeDtypeStruct((1,), I32),
            jax.ShapeDtypeStruct((block_limit, 8, 32 * TILES), I32),
        ],
        scratch_shapes=[pltpu.VMEM((shards * rows, HEAD), F32)],
        compiler_params=params(16),
        cost_estimate=pl.CostEstimate(
            flops=9000000000, bytes_accessed=3000000, transcendentals=0
        ),
        name="plan",
    )(page_map, span_order, listed_count, listed_lanes)


GROUPS = 4


def blend_kernel(
    me_ref, source, place, listed_lanes, received, mine, returned, ordered, blocks, sems
):
    shards, sent, _ = received.shape
    rows = listed_lanes.shape[1]
    own_pages = source.shape[0] // shards
    page_tokens = PAGE
    tokens = own_pages * page_tokens
    part = shards // GROUPS
    per_part = part * tokens // HEAD
    is_key = me_ref[0] % 2 == 0
    flat = received.reshape(shards * sent, HEAD)
    token = lax.broadcasted_iota(I32, (tokens, rows), 0)
    ones = jnp.ones((rows, HEAD), BF16)
    all_ones = jnp.ones((HEAD, HEAD), BF16)

    def send(g):
        span = pl.ds(g * per_part, per_part)
        return pltpu.make_async_copy(blocks.at[span], mine.at[span], sems.at[g])

    def group_step(g, most):
        for u in range(part):
            shard = g * part + u
            pages = []
            for page in range(own_pages):
                start = pl.multiple_of(source[shard * own_pages + page], page_tokens)
                pages.append(flat[pl.ds(start, page_tokens), :])
            cached = jnp.concatenate(pages, axis=0)
            pick = jnp.where(listed_lanes[pl.ds(shard, 1), :] == token, 1.0, 0.0).astype(BF16)
            fresh = jnp.concatenate([received[shard, 2 * rows + tokens :, :], ones], axis=1)
            found = jnp.dot(pick, fresh, preferred_element_type=F32)
            mixed = jnp.where(found[:, HEAD:] > 0.5, found[:, :HEAD], cached.astype(F32))
            start = pl.multiple_of(shard * tokens, 16)
            ordered[pl.ds(start, tokens), :] = mixed.astype(BF16)
            squares = jnp.dot((mixed * mixed).astype(BF16), all_ones, preferred_element_type=F32)
            most = jnp.maximum(most, jnp.max(squares.reshape(tokens // 8, 8, HEAD), axis=0))
        for u in range(per_part):
            at = g * per_part + u
            block = ordered[pl.ds(pl.multiple_of(at * HEAD, HEAD), HEAD), :]
            blocks[at] = jnp.where(is_key, block, block.T)
        send(g).start()
        return most

    most = lax.fori_loop(0, GROUPS, group_step, jnp.zeros((8, HEAD), F32))
    most = jnp.max(most, axis=0, keepdims=True)
    last = GROUPS * per_part
    blocks[last] = jnp.broadcast_to(most, (HEAD, HEAD)).astype(BF16)
    send_last = pltpu.make_async_copy(blocks.at[last], mine.at[last], sems.at[GROUPS])
    send_last.start()

    returned_pages = returned.shape[1] // page_tokens
    first = ((me_ref[0] // 2) % 2) * (own_pages - returned_pages)

    def return_step(shard, carry):
        for page in range(returned_pages):
            start = pl.multiple_of(place[shard * own_pages + first + page], page_tokens)
            span = slice(page * page_tokens, (page + 1) * page_tokens)
            returned[shard, span] = ordered[pl.ds(start, page_tokens), :]
        return carry

    lax.fori_loop(0, shards, return_step, 0, unroll=4)
    for g in range(GROUPS):
        send(g).wait()
    send_last.wait()


def blend(me, source, place, listed_lanes, received):
    shards, rows = listed_lanes.shape
    pages = source.shape[0]
    returned_pages = (pages // shards + 1) // 2
    smem = pl.BlockSpec(memory_space=SMEM)
    vmem = pl.BlockSpec(memory_space=VMEM)
    blocks = (pages * PAGE // HEAD + 1, HEAD, HEAD)
    return pl.pallas_call(
        blend_kernel,
        in_specs=[smem, smem, smem, vmem, vmem],
        out_specs=[pl.BlockSpec(memory_space=OUT_SPACE), vmem],
        out_shape=[
            jax.ShapeDtypeStruct(blocks, BF16),
            jax.ShapeDtypeStruct((shards, returned_pages * PAGE, HEAD), BF16),
        ],
        scratch_shapes=[
            pltpu.VMEM((pages * PAGE, HEAD), BF16),
            pltpu.VMEM(blocks, BF16),
            pltpu.SemaphoreType.DMA((GROUPS + 1,)),
        ],
        compiler_params=params(16),
        cost_estimate=pl.CostEstimate(
            flops=4000000000, bytes_accessed=3000000, transcendentals=0
        ),
        name="blend",
    )(me, source, place, listed_lanes, received)


SLACK = 60.0
LEAST = 2.0**-90


def attend_kernel(
    me_ref, tiles, block_count, positions, received, mine, other, out, scores, block
):
    core = me_ref[0] % 2
    out[...] = jnp.zeros_like(out)

    @pl.when(core == 0)
    def _():
        attend_blocks(tiles, block_count, positions, received, mine, other, out, scores, block)

    @pl.when(core != 0)
    def _():
        attend_blocks(tiles, block_count, positions, received, other, mine, out, scores, block)


def attend_blocks(
    tiles, block_count, positions, received, keys, values_t, out, scores, block
):
    chunks = scores.shape[0]
    per_chunk = CHUNK // HEAD
    shards = out.shape[0]
    rows = out.shape[1] // 2
    per_shard = rows // 16
    tokens = chunks * CHUNK // shards
    half = TILES * 16
    wide = 2 * half
    top = keys[chunks * per_chunk, :1, :1].astype(F32)
    ones = jnp.ones((16, max(BIG, per_chunk) * HEAD), BF16)

    def block_step(b, carry):
        first_tile = b * TILES
        for t in range(TILES):
            tile = tiles[first_tile + t]
            shard = tile // per_shard
            row = pl.multiple_of((tile - shard * per_shard) * 16, 16)
            block[t * 16 : (t + 1) * 16] = received[shard, pl.ds(row, 16), :]
            block[half + t * 16 : half + (t + 1) * 16] = received[shard, pl.ds(rows + row, 16), :]
        open_keys = (tiles[first_tile] // per_shard) * tokens
        seen_keys = (tiles[first_tile + TILES - 1] // per_shard + 1) * tokens
        seen_chunks = (seen_keys + CHUNK - 1) // CHUNK
        query = block[...]
        position = positions[b][:1]

        def score(start, count):
            products = lax.dot_general(
                keys[pl.ds(start, count)].reshape(count * HEAD, HEAD),
                query,
                (((1,), (1,)), ((), ())),
                preferred_element_type=F32,
            )
            return products * EXP2_SCALE

        def edge_score(start, count):
            found = score(start, count)
            key_position = start * HEAD + lax.broadcasted_iota(I32, (count * HEAD, wide), 0)
            return jnp.where(key_position <= position, found, MASKED)

        def add(start, count, found, shift, state):
            exps = jnp.exp2(found - shift).astype(BF16)
            value = [values_t[start + u] for u in range(count)]
            value = jnp.concatenate([jnp.concatenate(value, axis=1), ones[:, : count * HEAD]], axis=0)
            return state + jnp.dot(value, exps, preferred_element_type=F32)

        def finish(state):
            total = state[HEAD : HEAD + 1]
            result = state[:HEAD] / jnp.where(total > 0, total, 1.0)
            result = jnp.where(position >= 0, result, 0.0).T.astype(BF16)
            for t in range(TILES):
                tile = tiles[first_tile + t]
                shard = tile // per_shard
                row = pl.multiple_of((tile - shard * per_shard) * 16, 16)
                low = result[t * 16 : (t + 1) * 16]
                high = result[half + t * 16 : half + (t + 1) * 16]
                out[shard, pl.ds(row, 16), :] = low
                out[shard, pl.ds(rows + row, 16), :] = high
            return total

        nothing = jnp.zeros((HEAD + 16, wide), F32)
        squares = query.astype(F32)
        squares = lax.dot_general(
            jnp.ones((8, HEAD), BF16),
            (squares * squares).astype(BF16),
            (((1,), (1,)), ((), ())),
            preferred_element_type=F32,
        )
        bound = jnp.sqrt(squares[:1] * top) * (1.02 * EXP2_SCALE) - SLACK
        seen = seen_keys // PAGE
        big, mid, small = BIG * HEAD // PAGE, MID * HEAD // PAGE, SMALL * HEAD // PAGE
        big_steps = seen // big
        rest = seen - big_steps * big
        big_steps = big_steps + jnp.where(rest > mid + small, 1, 0)
        rest = jnp.where(rest > mid + small, 0, rest)
        mid_steps = jnp.where(rest > small, 1, 0)
        small_steps = jnp.where(rest > mid_steps * mid, 1, 0)
        open_steps = open_keys // (BIG * HEAD)
        mid_from = big_steps * BIG
        small_from = mid_from + mid_steps * MID

        def open_step(c, st):
            start = c * BIG
            return add(start, BIG, score(start, BIG), bound, st)

        def edge_step(start, count, st):
            return add(start, count, edge_score(start, count), bound, st)

        state = lax.fori_loop(0, open_steps, open_step, nothing)
        state = lax.fori_loop(
            open_steps, big_steps, lambda c, st: edge_step(c * BIG, BIG, st), state
        )
        state = lax.fori_loop(0, mid_steps, lambda c, st: edge_step(mid_from, MID, st), state)
        state = lax.fori_loop(
            0, small_steps, lambda c, st: edge_step(small_from, SMALL, st), state
        )
        total = finish(state)
        lowest = jnp.min(jnp.where(position >= 0, total, 1.0))

        @pl.when(lowest < LEAST)
        def _():
            def keep(chunk, best):
                found = edge_score(chunk * per_chunk, per_chunk)
                scores[chunk] = found
                return jnp.maximum(best, jnp.max(found.reshape(CHUNK // 8, 8, wide), axis=0))

            best = lax.fori_loop(0, seen_chunks, keep, jnp.full((8, wide), MASKED, F32))
            best = jnp.max(best, axis=0, keepdims=True)
            finish(
                lax.fori_loop(0, seen_chunks, lambda c, st: add(c * per_chunk, per_chunk, scores[c], best, st), nothing)
            )

        return carry

    lax.fori_loop(0, block_count[0], block_step, 0)


def attend(me, tiles, block_count, positions, received, mine, other, rows):
    shards = received.shape[0]
    smem = pl.BlockSpec(memory_space=SMEM)
    vmem = pl.BlockSpec(memory_space=VMEM)
    block = 2 * TILES * 16
    chunks = (mine.shape[0] - 1) * HEAD // CHUNK
    return pl.pallas_call(
        attend_kernel,
        in_specs=[smem, smem, smem, vmem, vmem, vmem, vmem],
        out_specs=vmem,
        out_shape=jax.ShapeDtypeStruct((shards, 2 * rows, HEAD), BF16),
        scratch_shapes=[
            pltpu.VMEM((chunks, CHUNK, block), F32),
            pltpu.VMEM((block, HEAD), BF16),
        ],
        compiler_params=params(28),
        cost_estimate=pl.CostEstimate(
            flops=16000000000, bytes_accessed=3000000, transcendentals=0
        ),
        name="attend",
    )(me, tiles, block_count, positions, received, mine, other)


def place_cache_kernel(received, keys, values):
    own_pages, page_tokens, _ = keys.shape
    shared = received.shape[1] // page_tokens
    for part, target in ((0, keys), (1, values)):
        for page in range(own_pages):
            source, at = (part, page) if page < shared else (2 + part, page - own_pages + shared)
            target[page] = received[source, at * page_tokens : (at + 1) * page_tokens]


def place_cache(received, own_pages, page_tokens):
    shards, sent, _ = received.shape
    group = shards // KV_HEADS
    cache = jax.ShapeDtypeStruct((own_pages, page_tokens, KV_HEADS * HEAD), BF16)
    spec = pl.BlockSpec((own_pages, page_tokens, HEAD), lambda h: (0, 0, h))
    return pl.pallas_call(
        place_cache_kernel,
        grid=(KV_HEADS,),
        in_specs=[pl.BlockSpec((group, sent, HEAD), lambda h: (h, 0, 0))],
        out_specs=[spec, spec],
        out_shape=[cache, cache],
        compiler_params=params(16),
        cost_estimate=pl.CostEstimate(
            flops=2500000000, bytes_accessed=3000000, transcendentals=0
        ),
        name="place_cache",
    )(received)


def place_attended_kernel(received, out):
    rows = out.shape[0]
    for j in range(received.shape[0]):
        for t in range(2):
            head = 2 * j + t
            out[:, head * HEAD : (head + 1) * HEAD] = received[j, t * rows : (t + 1) * rows]


def place_attended(received):
    shards, sent, _ = received.shape
    steps = 4
    rows, width = sent // 2, shards * 2 * HEAD
    return pl.pallas_call(
        place_attended_kernel,
        grid=(steps,),
        in_specs=[pl.BlockSpec((shards // steps, sent, HEAD), lambda h: (h, 0, 0))],
        out_specs=pl.BlockSpec((rows, width // steps), lambda h: (0, h)),
        out_shape=jax.ShapeDtypeStruct((rows, width), BF16),
        compiler_params=params(16),
        cost_estimate=pl.CostEstimate(flops=0, bytes_accessed=1600000, transcendentals=0),
        name="place_attended",
    )(received)


def exchange(blocks):
    return lax.all_to_all(blocks, "shard", 0, 0)


def shard_program(
    shards,
    paged_key_store,
    paged_value_store,
    paged_scale_store,
    page_map,
    span_order,
    listed_count,
    listed_index,
    listed_queries,
    selected_token_keys,
    selected_token_values,
):
    own_pages, page_tokens, _ = paged_key_store.shape
    rows = listed_queries.shape[0]
    me = lax.axis_index("shard").astype(I32).reshape(1)

    received = exchange(
        prepare(
            me,
            page_map,
            span_order,
            listed_index,
            paged_scale_store.transpose(1, 2, 0),
            listed_queries,
            paged_key_store,
            paged_value_store,
            selected_token_keys,
            selected_token_values,
            shards,
        )
    )

    listed = jnp.arange(rows, dtype=I32)[None, :] < listed_count[:, None]
    listed_lanes = jnp.where(listed, listed_index.reshape(shards, rows), -1)
    source, place, tiles, block_count, positions = plan(
        page_map, span_order, listed_count, listed_lanes
    )

    mine, returned = blend(me, source, place, listed_lanes, received)
    other = lax.ppermute(mine, "shard", [(i, i ^ 1) for i in range(shards)])
    received_cache = exchange(returned)
    attended = attend(me, tiles, block_count, positions, received, mine, other, rows)
    mixed_keys, mixed_values = place_cache(received_cache, own_pages, page_tokens)
    return mixed_keys, mixed_values, place_attended(exchange(attended))


def solution(mesh):
    split = ("req", "shard")
    in_specs = (
        P(split, None, None),
        P(split, None, None),
        P(split, None, None),
        P("req"),
        P("req"),
        P("req"),
        P("req"),
        P(split, None),
        P(split, None),
        P(split, None),
    )
    out_specs = (P(split, None, None), P(split, None, None), P(split, None))
    return jax.shard_map(
        functools.partial(shard_program, mesh.shape["shard"]),
        mesh=mesh,
        in_specs=in_specs,
        out_specs=out_specs,
        check_vma=False,
    )
```

```python
import functools

import jax
import jax.numpy as jnp
import numpy as np
from jax import lax
from jax.experimental import pallas as pl
from jax.experimental.pallas import tpu as pltpu
from jax.sharding import PartitionSpec as P

HEAD = 128
KV_HEADS = 8
SPAN_LEN = 704
ROPE_BASE = 1000000.0
MASKED = -1e30
VMEM_MIB = 56
UNIT = 8
UNITS = 32
CHUNK = 1408
PAGE = 16
BIG = 22
MID = 11
SMALL = 4
EXP2_SCALE = float(HEAD**-0.5 / np.log(2.0))

BF16 = jnp.bfloat16
F32 = jnp.float32
I32 = jnp.int32
SMEM = pltpu.SMEM
VMEM = pltpu.VMEM
OUT_SPACE = pltpu.HBM


def rope_frequency():
    half = HEAD // 2
    frequency = ROPE_BASE ** (-(np.arange(half, dtype=np.float64) * 2.0) / HEAD)
    return np.concatenate([frequency, frequency]).astype(np.float32)[None, :]


def rope_tables(position, frequency):
    angles = position * frequency
    lane = lax.broadcasted_iota(I32, angles.shape, 1)
    sine = jnp.sin(angles)
    return jnp.cos(angles), jnp.where(lane < HEAD // 2, -sine, sine)


def rotate(x, cosine, sine):
    return x * cosine + pltpu.roll(x, HEAD // 2, 1) * sine


def params(mib, **more):
    return pltpu.CompilerParams(vmem_limit_bytes=mib * 1024 * 1024, **more)


def prepare_kernel(
    me_ref,
    page_map,
    span_order,
    listed_index,
    scale,
    frequency,
    queries_in,
    keys_in,
    values_in,
    fresh_keys_in,
    fresh_values_in,
    out,
    queries,
    keys,
    values,
    fresh_keys,
    fresh_values,
    blocks,
    slots,
    positions,
    shift_cos,
    shift_sin,
    in_sems,
    out_sems,
):
    me = me_ref[0]
    own_pages, page_tokens, _ = keys.shape
    rows = fresh_keys.shape[0]
    group = blocks.shape[0] // KV_HEADS
    span_count = span_order.shape[0]
    per_span = page_map.shape[0] // span_count
    tokens = own_pages * page_tokens
    arrivals = [
        pltpu.make_async_copy(source, target, in_sems.at[i])
        for i, (source, target) in enumerate(
            (
                (queries_in, queries),
                (keys_in, keys),
                (values_in, values),
                (fresh_keys_in, fresh_keys),
                (fresh_values_in, fresh_values),
            )
        )
    ]
    for arrival in arrivals:
        arrival.start()

    for c in range(rows):
        position = (me * tokens + listed_index[me * rows + c]).astype(F32)
        positions[c : c + 1, :] = jnp.full((1, HEAD), position, F32)
    cosine, sine = rope_tables(positions[...], frequency[...])
    shift = lax.broadcasted_iota(I32, (span_count, HEAD), 0) * SPAN_LEN
    shift_cos[...], shift_sin[...] = rope_tables(shift.astype(F32), frequency[...])
    first = me * own_pages
    for slot in range(span_count):
        start = span_order[slot] * per_span

        def note(p, carry):
            place = page_map[start + p] - first
            inside = (place >= 0) & (place < own_pages)
            slots[jnp.where(inside, place, own_pages)] = slot
            return carry

        lax.fori_loop(0, per_span, note, 0, unroll=11)
    page_slots = [slots[page] for page in range(own_pages)]
    for arrival in arrivals:
        arrival.wait()

    departures = []
    for head in range(KV_HEADS):
        lanes = slice(head * HEAD, (head + 1) * HEAD)
        outs = [head * group + j for j in range(group)]
        for j in range(group):
            for t in range(2):
                at = (2 * (head * group + j) + t) * HEAD
                x = queries[:, at : at + HEAD].astype(F32)
                blocks[outs[j], t * rows : (t + 1) * rows] = rotate(x, cosine, sine).astype(BF16)
        base = 2 * rows
        for page in range(own_pages):
            page_cos = shift_cos[pl.ds(page_slots[page], 1), :]
            page_sin = shift_sin[pl.ds(page_slots[page], 1), :]
            span = slice(base + page * page_tokens, base + (page + 1) * page_tokens)
            key = keys[page, :, lanes].astype(F32) * scale[0, head, page]
            key = rotate(key, page_cos, page_sin).astype(BF16)
            value = (values[page, :, lanes].astype(F32) * scale[1, head, page]).astype(BF16)
            for j in range(group):
                blocks[outs[j], span] = value if j % 2 else key
        key = rotate(fresh_keys[:, lanes].astype(F32), cosine, sine).astype(BF16)
        value = fresh_values[:, lanes]
        for j in range(group):
            blocks[outs[j], base + tokens :] = value if j % 2 else key
        span = pl.ds(head * group, group)
        departures.append(
            pltpu.make_async_copy(blocks.at[span], out.at[span], out_sems.at[head])
        )
        departures[-1].start()
    for departure in departures:
        departure.wait()


def prepare(
    me,
    page_map,
    span_order,
    listed_index,
    scale,
    queries,
    keys,
    values,
    fresh_keys,
    fresh_values,
    shards,
):
    own_pages, page_tokens, _ = keys.shape
    rows, width = queries.shape
    sent = 3 * rows + own_pages * page_tokens
    smem = pl.BlockSpec(memory_space=SMEM)
    vmem = pl.BlockSpec(memory_space=VMEM)
    anywhere = pl.BlockSpec(memory_space=pl.ANY)
    arrays = (queries, keys, values, fresh_keys, fresh_values)
    return pl.pallas_call(
        prepare_kernel,
        in_specs=[smem] * 5 + [vmem] + [anywhere] * 5,
        out_specs=pl.BlockSpec(memory_space=OUT_SPACE),
        out_shape=jax.ShapeDtypeStruct((shards, sent, HEAD), BF16),
        scratch_shapes=[pltpu.VMEM(a.shape, a.dtype) for a in arrays]
        + [
            pltpu.VMEM((shards, sent, HEAD), BF16),
            pltpu.SMEM((own_pages + 1,), I32),
            pltpu.VMEM((rows, HEAD), F32),
            pltpu.VMEM((span_order.shape[0], HEAD), F32),
            pltpu.VMEM((span_order.shape[0], HEAD), F32),
            pltpu.SemaphoreType.DMA((len(arrays),)),
            pltpu.SemaphoreType.DMA((KV_HEADS,)),
        ],
        compiler_params=params(VMEM_MIB),
        cost_estimate=pl.CostEstimate(
            flops=5000000000, bytes_accessed=4300000, transcendentals=0
        ),
        name="prepare",
    )(
        me,
        page_map,
        span_order,
        listed_index,
        scale,
        jnp.asarray(rope_frequency()),
        *arrays,
    )


def plan_kernel(
    page_map,
    span_order,
    listed_count,
    listed_lanes,
    source,
    place,
    tiles,
    block_count,
    positions,
    row_position,
):
    shards, rows = listed_lanes.shape
    pages = page_map.shape[0]
    own_pages = pages // shards
    page_tokens = PAGE
    tokens = own_pages * page_tokens
    sent = tokens + 3 * rows
    span_count = span_order.shape[0]
    per_span = pages // span_count

    for slot in range(span_count):
        start = span_order[slot] * per_span

        def note(p, carry):
            stored = page_map[start + p]
            logical = slot * per_span + p
            owner = stored // own_pages
            within = stored - owner * own_pages
            source[logical] = owner * sent + 2 * rows + within * page_tokens
            place[stored] = logical * page_tokens
            return carry

        lax.fori_loop(0, per_span, note, 0, unroll=4)

    def count_tiles(shard, total):
        return total + (listed_count[shard] + UNIT - 1) // UNIT

    total = lax.fori_loop(0, shards, count_tiles, 0)
    blocks = (total + UNITS - 1) // UNITS
    block_count[0] = blocks
    for k in range(UNITS):
        tiles[k] = 0

    def list_tiles(shard, filled):
        count = listed_count[shard]
        for k in range(rows // UNIT):
            tiles[filled] = shard * 8 + k
            filled = filled + jnp.where(count > UNIT * k, 1, 0)
        return filled

    lax.fori_loop(0, shards, list_tiles, blocks * UNITS - total)

    diagonal = lax.broadcasted_iota(I32, (rows, rows), 0) == lax.broadcasted_iota(
        I32, (rows, rows), 1
    )

    def fill(shard, carry):
        listed = listed_lanes[pl.ds(shard, 1), :].astype(F32)
        offset = jnp.sum(jnp.where(diagonal, listed, 0.0), axis=1, keepdims=True)
        position = jnp.where(offset < 0.0, -1.0, offset + (shard * tokens).astype(F32))
        start = pl.multiple_of(shard * rows, 16)
        row_position[pl.ds(start, rows), :] = jnp.broadcast_to(position, (rows, HEAD))
        return carry

    lax.fori_loop(0, shards, fill, 0)

    def place_positions(b, carry):
        lanes = []
        for t in range(0, UNITS, HEAD // UNIT):
            found = []
            for u in range(t, t + HEAD // UNIT):
                code = tiles[b * UNITS + u]
                start = pl.multiple_of((code >> 3) * rows + (code & 7) * UNIT, UNIT)
                found.append(row_position[pl.ds(start, UNIT), :])
            lanes.append(jnp.concatenate(found, axis=0).T[:8])
        positions[b] = jnp.concatenate(lanes + lanes, axis=1).astype(I32)
        return carry

    lax.fori_loop(0, blocks, place_positions, 0)


def plan(page_map, span_order, listed_count, listed_lanes):
    shards, rows = listed_lanes.shape
    smem = pl.BlockSpec(memory_space=SMEM)
    vmem = pl.BlockSpec(memory_space=VMEM)
    pages = page_map.shape[0]
    block_limit = pl.cdiv(shards * (rows // UNIT), UNITS)
    return pl.pallas_call(
        plan_kernel,
        in_specs=[smem, smem, smem, vmem],
        out_specs=[smem, smem, smem, smem, vmem],
        out_shape=[
            jax.ShapeDtypeStruct((pages,), I32),
            jax.ShapeDtypeStruct((pages,), I32),
            jax.ShapeDtypeStruct(((block_limit + 1) * UNITS,), I32),
            jax.ShapeDtypeStruct((1,), I32),
            jax.ShapeDtypeStruct((block_limit, 8, 2 * UNIT * UNITS), I32),
        ],
        scratch_shapes=[pltpu.VMEM((shards * rows, HEAD), F32)],
        compiler_params=params(16),
        cost_estimate=pl.CostEstimate(
            flops=9000000000, bytes_accessed=3000000, transcendentals=0
        ),
        name="plan",
    )(page_map, span_order, listed_count, listed_lanes)


GROUPS = 4


def blend_kernel(
    me_ref, source, place, listed_lanes, received, mine, returned, ordered, blocks, sems
):
    shards, sent, _ = received.shape
    rows = listed_lanes.shape[1]
    own_pages = source.shape[0] // shards
    page_tokens = PAGE
    tokens = own_pages * page_tokens
    part = shards // GROUPS
    per_part = part * tokens // HEAD
    is_key = me_ref[0] % 2 == 0
    flat = received.reshape(shards * sent, HEAD)
    token = lax.broadcasted_iota(I32, (tokens, rows), 0)
    ones = jnp.ones((rows, HEAD), BF16)
    all_ones = jnp.ones((HEAD, HEAD), BF16)

    def send(g):
        span = pl.ds(g * per_part, per_part)
        return pltpu.make_async_copy(blocks.at[span], mine.at[span], sems.at[g])

    def group_step(g, most):
        for u in range(part):
            shard = g * part + u
            pages = []
            for page in range(own_pages):
                start = pl.multiple_of(source[shard * own_pages + page], page_tokens)
                pages.append(flat[pl.ds(start, page_tokens), :])
            cached = jnp.concatenate(pages, axis=0)
            pick = jnp.where(listed_lanes[pl.ds(shard, 1), :] == token, 1.0, 0.0).astype(BF16)
            fresh = jnp.concatenate([received[shard, 2 * rows + tokens :, :], ones], axis=1)
            found = jnp.dot(pick, fresh, preferred_element_type=F32)
            mixed = jnp.where(found[:, HEAD:] > 0.5, found[:, :HEAD], cached.astype(F32))
            start = pl.multiple_of(shard * tokens, 16)
            ordered[pl.ds(start, tokens), :] = mixed.astype(BF16)
            squares = jnp.dot((mixed * mixed).astype(BF16), all_ones, preferred_element_type=F32)
            most = jnp.maximum(most, jnp.max(squares.reshape(tokens // 8, 8, HEAD), axis=0))
        for u in range(per_part):
            at = g * per_part + u
            block = ordered[pl.ds(pl.multiple_of(at * HEAD, HEAD), HEAD), :]
            blocks[at] = jnp.where(is_key, block, block.T)
        send(g).start()
        return most

    most = lax.fori_loop(0, GROUPS, group_step, jnp.zeros((8, HEAD), F32))
    most = jnp.max(most, axis=0, keepdims=True)
    last = GROUPS * per_part
    blocks[last] = jnp.broadcast_to(most, (HEAD, HEAD)).astype(BF16)
    send_last = pltpu.make_async_copy(blocks.at[last], mine.at[last], sems.at[GROUPS])
    send_last.start()

    returned_pages = returned.shape[1] // page_tokens
    first = ((me_ref[0] // 2) % 2) * (own_pages - returned_pages)

    def return_step(shard, carry):
        for page in range(returned_pages):
            start = pl.multiple_of(place[shard * own_pages + first + page], page_tokens)
            span = slice(page * page_tokens, (page + 1) * page_tokens)
            returned[shard, span] = ordered[pl.ds(start, page_tokens), :]
        return carry

    lax.fori_loop(0, shards, return_step, 0, unroll=4)
    for g in range(GROUPS):
        send(g).wait()
    send_last.wait()


def blend(me, source, place, listed_lanes, received):
    shards, rows = listed_lanes.shape
    pages = source.shape[0]
    returned_pages = (pages // shards + 1) // 2
    smem = pl.BlockSpec(memory_space=SMEM)
    vmem = pl.BlockSpec(memory_space=VMEM)
    blocks = (pages * PAGE // HEAD + 1, HEAD, HEAD)
    return pl.pallas_call(
        blend_kernel,
        in_specs=[smem, smem, smem, vmem, vmem],
        out_specs=[pl.BlockSpec(memory_space=OUT_SPACE), vmem],
        out_shape=[
            jax.ShapeDtypeStruct(blocks, BF16),
            jax.ShapeDtypeStruct((shards, returned_pages * PAGE, HEAD), BF16),
        ],
        scratch_shapes=[
            pltpu.VMEM((pages * PAGE, HEAD), BF16),
            pltpu.VMEM(blocks, BF16),
            pltpu.SemaphoreType.DMA((GROUPS + 1,)),
        ],
        compiler_params=params(16),
        cost_estimate=pl.CostEstimate(
            flops=4000000000, bytes_accessed=3000000, transcendentals=0
        ),
        name="blend",
    )(me, source, place, listed_lanes, received)


SLACK = 60.0
LEAST = 2.0**-90


def attend_kernel(
    me_ref, tiles, block_count, positions, received, mine, other, out, scores, block, wide_out
):
    core = me_ref[0] % 2
    wide_out[...] = jnp.zeros_like(wide_out)

    @pl.when(core == 0)
    def _():
        attend_blocks(
            tiles, block_count, positions, received, mine, other, wide_out, scores, block
        )

    @pl.when(core != 0)
    def _():
        attend_blocks(
            tiles, block_count, positions, received, other, mine, wide_out, scores, block
        )

    out[...] = wide_out[...].astype(BF16)


def attend_blocks(
    tiles, block_count, positions, received, keys, values_t, out, scores, block
):
    chunks = scores.shape[0]
    per_chunk = CHUNK // HEAD
    shards = out.shape[0]
    rows = out.shape[1] // 2
    tokens = chunks * CHUNK // shards
    half = UNITS * UNIT
    wide = 2 * half
    top = keys[chunks * per_chunk, :1, :1].astype(F32)
    ones = jnp.ones((16, max(BIG, per_chunk) * HEAD), BF16)

    def block_step(b, carry):
        first_tile = b * UNITS
        codes = [tiles[first_tile + t] for t in range(UNITS)]
        for t in range(UNITS):
            shard, unit = codes[t] >> 3, codes[t] & 7
            odd = (unit & 1) == 1
            for side in range(2):
                row = pl.multiple_of(side * rows + (unit >> 1) * 16, 16)
                pair = received[shard, pl.ds(row, 16), :].astype(F32)
                at = side * half + t * UNIT
                block[at : at + UNIT] = jnp.where(odd, pair[UNIT:], pair[:UNIT])
        open_keys = (codes[0] >> 3) * tokens
        seen_keys = ((codes[UNITS - 1] >> 3) + 1) * tokens
        seen_chunks = (seen_keys + CHUNK - 1) // CHUNK
        query = block[...].astype(BF16)
        position = positions[b][:1]

        def score(start, count):
            products = lax.dot_general(
                keys[pl.ds(start, count)].reshape(count * HEAD, HEAD),
                query,
                (((1,), (1,)), ((), ())),
                preferred_element_type=F32,
            )
            return products * EXP2_SCALE

        def edge_score(start, count):
            found = score(start, count)
            key_position = start * HEAD + lax.broadcasted_iota(I32, (count * HEAD, wide), 0)
            return jnp.where(key_position <= position, found, MASKED)

        def add(start, count, found, shift, state):
            exps = jnp.exp2(found - shift).astype(BF16)
            value = [values_t[start + u] for u in range(count)]
            value = jnp.concatenate([jnp.concatenate(value, axis=1), ones[:, : count * HEAD]], axis=0)
            return state + jnp.dot(value, exps, preferred_element_type=F32)

        def finish(state):
            total = state[HEAD : HEAD + 1]
            result = state[:HEAD] / jnp.where(total > 0, total, 1.0)
            result = jnp.where(position >= 0, result, 0.0).T
            for t in range(UNITS):
                shard, unit = codes[t] >> 3, codes[t] & 7
                for side in range(2):
                    row = pl.multiple_of(side * rows + unit * UNIT, UNIT)
                    at = side * half + t * UNIT
                    out[shard, pl.ds(row, UNIT), :] = result[at : at + UNIT]
            return total

        nothing = jnp.zeros((HEAD + 16, wide), F32)
        squares = query.astype(F32)
        squares = lax.dot_general(
            jnp.ones((8, HEAD), BF16),
            (squares * squares).astype(BF16),
            (((1,), (1,)), ((), ())),
            preferred_element_type=F32,
        )
        bound = jnp.sqrt(squares[:1] * top) * (1.02 * EXP2_SCALE) - SLACK
        seen = seen_keys // PAGE
        big, mid, small = BIG * HEAD // PAGE, MID * HEAD // PAGE, SMALL * HEAD // PAGE
        big_steps = seen // big
        rest = seen - big_steps * big
        big_steps = big_steps + jnp.where(rest > mid + small, 1, 0)
        rest = jnp.where(rest > mid + small, 0, rest)
        mid_steps = jnp.where(rest > small, 1, 0)
        small_steps = jnp.where(rest > mid_steps * mid, 1, 0)
        open_steps = open_keys // (BIG * HEAD)
        mid_from = big_steps * BIG
        small_from = mid_from + mid_steps * MID

        def open_step(c, st):
            start = c * BIG
            return add(start, BIG, score(start, BIG), bound, st)

        def edge_step(start, count, st):
            return add(start, count, edge_score(start, count), bound, st)

        state = lax.fori_loop(0, open_steps, open_step, nothing)
        state = lax.fori_loop(
            open_steps, big_steps, lambda c, st: edge_step(c * BIG, BIG, st), state
        )
        state = lax.fori_loop(0, mid_steps, lambda c, st: edge_step(mid_from, MID, st), state)
        state = lax.fori_loop(
            0, small_steps, lambda c, st: edge_step(small_from, SMALL, st), state
        )
        total = finish(state)
        lowest = jnp.min(jnp.where(position >= 0, total, 1.0))

        @pl.when(lowest < LEAST)
        def _():
            def keep(chunk, best):
                found = edge_score(chunk * per_chunk, per_chunk)
                scores[chunk] = found
                return jnp.maximum(best, jnp.max(found.reshape(CHUNK // 8, 8, wide), axis=0))

            best = lax.fori_loop(0, seen_chunks, keep, jnp.full((8, wide), MASKED, F32))
            best = jnp.max(best, axis=0, keepdims=True)
            finish(
                lax.fori_loop(0, seen_chunks, lambda c, st: add(c * per_chunk, per_chunk, scores[c], best, st), nothing)
            )

        return carry

    lax.fori_loop(0, block_count[0], block_step, 0)


def attend(me, tiles, block_count, positions, received, mine, other, rows):
    shards = received.shape[0]
    smem = pl.BlockSpec(memory_space=SMEM)
    vmem = pl.BlockSpec(memory_space=VMEM)
    block = 2 * UNITS * UNIT
    chunks = (mine.shape[0] - 1) * HEAD // CHUNK
    return pl.pallas_call(
        attend_kernel,
        in_specs=[smem, smem, smem, vmem, vmem, vmem, vmem],
        out_specs=vmem,
        out_shape=jax.ShapeDtypeStruct((shards, 2 * rows, HEAD), BF16),
        scratch_shapes=[
            pltpu.VMEM((chunks, CHUNK, block), F32),
            pltpu.VMEM((block, HEAD), F32),
            pltpu.VMEM((shards, 2 * rows, HEAD), F32),
        ],
        compiler_params=params(28),
        cost_estimate=pl.CostEstimate(
            flops=16000000000, bytes_accessed=3000000, transcendentals=0
        ),
        name="attend",
    )(me, tiles, block_count, positions, received, mine, other)


def place_cache_kernel(received, keys, values):
    own_pages, page_tokens, _ = keys.shape
    shared = received.shape[1] // page_tokens
    for part, target in ((0, keys), (1, values)):
        for page in range(own_pages):
            source, at = (part, page) if page < shared else (2 + part, page - own_pages + shared)
            target[page] = received[source, at * page_tokens : (at + 1) * page_tokens]


def place_cache(received, own_pages, page_tokens):
    shards, sent, _ = received.shape
    group = shards // KV_HEADS
    cache = jax.ShapeDtypeStruct((own_pages, page_tokens, KV_HEADS * HEAD), BF16)
    spec = pl.BlockSpec((own_pages, page_tokens, HEAD), lambda h: (0, 0, h))
    return pl.pallas_call(
        place_cache_kernel,
        grid=(KV_HEADS,),
        in_specs=[pl.BlockSpec((group, sent, HEAD), lambda h: (h, 0, 0))],
        out_specs=[spec, spec],
        out_shape=[cache, cache],
        compiler_params=params(16),
        cost_estimate=pl.CostEstimate(
            flops=2500000000, bytes_accessed=3000000, transcendentals=0
        ),
        name="place_cache",
    )(received)


def place_attended_kernel(received, out):
    rows = out.shape[0]
    for j in range(received.shape[0]):
        for t in range(2):
            head = 2 * j + t
            out[:, head * HEAD : (head + 1) * HEAD] = received[j, t * rows : (t + 1) * rows]


def place_attended(received):
    shards, sent, _ = received.shape
    steps = 4
    rows, width = sent // 2, shards * 2 * HEAD
    return pl.pallas_call(
        place_attended_kernel,
        grid=(steps,),
        in_specs=[pl.BlockSpec((shards // steps, sent, HEAD), lambda h: (h, 0, 0))],
        out_specs=pl.BlockSpec((rows, width // steps), lambda h: (0, h)),
        out_shape=jax.ShapeDtypeStruct((rows, width), BF16),
        compiler_params=params(16),
        cost_estimate=pl.CostEstimate(flops=0, bytes_accessed=1600000, transcendentals=0),
        name="place_attended",
    )(received)


def exchange(blocks):
    return lax.all_to_all(blocks, "shard", 0, 0)


def shard_program(
    shards,
    paged_key_store,
    paged_value_store,
    paged_scale_store,
    page_map,
    span_order,
    listed_count,
    listed_index,
    listed_queries,
    selected_token_keys,
    selected_token_values,
):
    own_pages, page_tokens, _ = paged_key_store.shape
    rows = listed_queries.shape[0]
    me = lax.axis_index("shard").astype(I32).reshape(1)

    received = exchange(
        prepare(
            me,
            page_map,
            span_order,
            listed_index,
            paged_scale_store.transpose(1, 2, 0),
            listed_queries,
            paged_key_store,
            paged_value_store,
            selected_token_keys,
            selected_token_values,
            shards,
        )
    )

    listed = jnp.arange(rows, dtype=I32)[None, :] < listed_count[:, None]
    listed_lanes = jnp.where(listed, listed_index.reshape(shards, rows), -1)
    source, place, tiles, block_count, positions = plan(
        page_map, span_order, listed_count, listed_lanes
    )

    mine, returned = blend(me, source, place, listed_lanes, received)
    other = lax.ppermute(mine, "shard", [(i, i ^ 1) for i in range(shards)])
    received_cache = exchange(returned)
    attended = attend(me, tiles, block_count, positions, received, mine, other, rows)
    mixed_keys, mixed_values = place_cache(received_cache, own_pages, page_tokens)
    return mixed_keys, mixed_values, place_attended(exchange(attended))


def solution(mesh):
    split = ("req", "shard")
    in_specs = (
        P(split, None, None),
        P(split, None, None),
        P(split, None, None),
        P("req"),
        P("req"),
        P("req"),
        P("req"),
        P(split, None),
        P(split, None),
        P(split, None),
    )
    out_specs = (P(split, None, None), P(split, None, None), P(split, None))
    return jax.shard_map(
        functools.partial(shard_program, mesh.shape["shard"]),
        mesh=mesh,
        in_specs=in_specs,
        out_specs=out_specs,
        check_vma=False,
    )
```

```python
import functools

import jax
import jax.numpy as jnp
import numpy as np
from jax import lax
from jax.experimental import pallas as pl
from jax.experimental.pallas import tpu as pltpu
from jax.sharding import PartitionSpec as P

HEAD = 128
KV_HEADS = 8
SPAN_LEN = 704
ROPE_BASE = 1000000.0
MASKED = -1e30
VMEM_MIB = 56
UNIT = 8
UNITS = 32
CHUNK = 1408
PAGE = 16
EXP2_SCALE = float(HEAD**-0.5 / np.log(2.0))

BF16 = jnp.bfloat16
F32 = jnp.float32
I32 = jnp.int32
SMEM = pltpu.SMEM
VMEM = pltpu.VMEM
OUT_SPACE = pltpu.HBM


def rope_frequency():
    half = HEAD // 2
    frequency = ROPE_BASE ** (-(np.arange(half, dtype=np.float64) * 2.0) / HEAD)
    return np.concatenate([frequency, frequency]).astype(np.float32)[None, :]


def rope_tables(position, frequency):
    angles = position * frequency
    lane = lax.broadcasted_iota(I32, angles.shape, 1)
    sine = jnp.sin(angles)
    return jnp.cos(angles), jnp.where(lane < HEAD // 2, -sine, sine)


def rotate(x, cosine, sine):
    return x * cosine + pltpu.roll(x, HEAD // 2, 1) * sine


def params(mib, **more):
    return pltpu.CompilerParams(vmem_limit_bytes=mib * 1024 * 1024, **more)


def prepare_kernel(
    me_ref,
    page_map,
    span_order,
    listed_index,
    scale,
    frequency,
    queries_in,
    keys_in,
    values_in,
    fresh_keys_in,
    fresh_values_in,
    out,
    queries,
    keys,
    values,
    fresh_keys,
    fresh_values,
    blocks,
    slots,
    positions,
    shift_cos,
    shift_sin,
    in_sems,
    out_sems,
):
    me = me_ref[0]
    own_pages, page_tokens, _ = keys.shape
    rows = fresh_keys.shape[0]
    group = blocks.shape[0] // KV_HEADS
    span_count = span_order.shape[0]
    per_span = page_map.shape[0] // span_count
    tokens = own_pages * page_tokens
    arrivals = [
        pltpu.make_async_copy(source, target, in_sems.at[i])
        for i, (source, target) in enumerate(
            (
                (keys_in, keys),
                (values_in, values),
                (fresh_keys_in, fresh_keys),
                (fresh_values_in, fresh_values),
            )
        )
    ]
    query_arrivals = []
    for head in range(KV_HEADS):
        wide = queries.shape[1] // KV_HEADS
        lanes = pl.ds(head * wide, wide)
        query_arrivals.append(
            pltpu.make_async_copy(
                queries_in.at[:, lanes], queries.at[:, lanes], in_sems.at[len(arrivals) + head]
            )
        )
    for arrival in arrivals + query_arrivals:
        arrival.start()

    for c in range(rows):
        position = (me * tokens + listed_index[me * rows + c]).astype(F32)
        positions[c : c + 1, :] = jnp.full((1, HEAD), position, F32)
    cosine, sine = rope_tables(positions[...], frequency[...])
    shift = lax.broadcasted_iota(I32, (span_count, HEAD), 0) * SPAN_LEN
    shift_cos[...], shift_sin[...] = rope_tables(shift.astype(F32), frequency[...])
    first = me * own_pages
    for slot in range(span_count):
        start = span_order[slot] * per_span

        def note(p, carry):
            place = page_map[start + p] - first
            inside = (place >= 0) & (place < own_pages)
            slots[jnp.where(inside, place, own_pages)] = slot
            return carry

        lax.fori_loop(0, per_span, note, 0, unroll=11)
    page_slots = [slots[page] for page in range(own_pages)]
    for arrival in arrivals:
        arrival.wait()

    departures = []
    for head in range(KV_HEADS):
        lanes = slice(head * HEAD, (head + 1) * HEAD)
        outs = [head * group + j for j in range(group)]
        query_arrivals[head].wait()
        for j in range(group):
            for t in range(2):
                at = (2 * (head * group + j) + t) * HEAD
                x = queries[:, at : at + HEAD].astype(F32)
                blocks[outs[j], t * rows : (t + 1) * rows] = rotate(x, cosine, sine).astype(BF16)
        base = 2 * rows
        for page in range(own_pages):
            page_cos = shift_cos[pl.ds(page_slots[page], 1), :]
            page_sin = shift_sin[pl.ds(page_slots[page], 1), :]
            span = slice(base + page * page_tokens, base + (page + 1) * page_tokens)
            key = keys[page, :, lanes].astype(F32) * scale[0, head, page]
            key = rotate(key, page_cos, page_sin).astype(BF16)
            value = (values[page, :, lanes].astype(F32) * scale[1, head, page]).astype(BF16)
            for j in range(group):
                blocks[outs[j], span] = value if j % 2 else key
        key = rotate(fresh_keys[:, lanes].astype(F32), cosine, sine).astype(BF16)
        value = fresh_values[:, lanes]
        for j in range(group):
            blocks[outs[j], base + tokens :] = value if j % 2 else key
        span = pl.ds(head * group, group)
        departures.append(
            pltpu.make_async_copy(blocks.at[span], out.at[span], out_sems.at[head])
        )
        departures[-1].start()
    for departure in departures:
        departure.wait()


def prepare(
    me,
    page_map,
    span_order,
    listed_index,
    scale,
    queries,
    keys,
    values,
    fresh_keys,
    fresh_values,
    shards,
):
    own_pages, page_tokens, _ = keys.shape
    rows, width = queries.shape
    sent = 3 * rows + own_pages * page_tokens
    smem = pl.BlockSpec(memory_space=SMEM)
    vmem = pl.BlockSpec(memory_space=VMEM)
    anywhere = pl.BlockSpec(memory_space=pl.ANY)
    arrays = (queries, keys, values, fresh_keys, fresh_values)
    return pl.pallas_call(
        prepare_kernel,
        in_specs=[smem] * 5 + [vmem] + [anywhere] * 5,
        out_specs=pl.BlockSpec(memory_space=OUT_SPACE),
        out_shape=jax.ShapeDtypeStruct((shards, sent, HEAD), BF16),
        scratch_shapes=[pltpu.VMEM(a.shape, a.dtype) for a in arrays]
        + [
            pltpu.VMEM((shards, sent, HEAD), BF16),
            pltpu.SMEM((own_pages + 1,), I32),
            pltpu.VMEM((rows, HEAD), F32),
            pltpu.VMEM((span_order.shape[0], HEAD), F32),
            pltpu.VMEM((span_order.shape[0], HEAD), F32),
            pltpu.SemaphoreType.DMA((len(arrays) - 1 + KV_HEADS,)),
            pltpu.SemaphoreType.DMA((KV_HEADS,)),
        ],
        compiler_params=params(VMEM_MIB),
        cost_estimate=pl.CostEstimate(
            flops=5000000000, bytes_accessed=4300000, transcendentals=0
        ),
        name="prepare",
    )(
        me,
        page_map,
        span_order,
        listed_index,
        scale,
        jnp.asarray(rope_frequency()),
        *arrays,
    )


def plan_kernel(
    page_map,
    span_order,
    listed_count,
    listed_lanes,
    source,
    place,
    tiles,
    block_count,
    positions,
    row_position,
):
    shards, rows = listed_lanes.shape
    pages = page_map.shape[0]
    own_pages = pages // shards
    page_tokens = PAGE
    tokens = own_pages * page_tokens
    sent = tokens + 3 * rows
    span_count = span_order.shape[0]
    per_span = pages // span_count

    for slot in range(span_count):
        start = span_order[slot] * per_span

        def note(p, carry):
            stored = page_map[start + p]
            logical = slot * per_span + p
            owner = stored // own_pages
            within = stored - owner * own_pages
            source[logical] = owner * sent + 2 * rows + within * page_tokens
            place[stored] = logical * page_tokens
            return carry

        lax.fori_loop(0, per_span, note, 0, unroll=4)

    def count_tiles(shard, total):
        return total + (listed_count[shard] + UNIT - 1) // UNIT

    total = lax.fori_loop(0, shards, count_tiles, 0)
    blocks = (total + UNITS - 1) // UNITS
    block_count[0] = blocks
    for k in range(UNITS):
        tiles[k] = 0

    def list_tiles(shard, filled):
        count = listed_count[shard]
        for k in range(rows // UNIT):
            tiles[filled] = shard * 8 + k
            filled = filled + jnp.where(count > UNIT * k, 1, 0)
        return filled

    lax.fori_loop(0, shards, list_tiles, blocks * UNITS - total)

    diagonal = lax.broadcasted_iota(I32, (rows, rows), 0) == lax.broadcasted_iota(
        I32, (rows, rows), 1
    )

    def fill(shard, carry):
        listed = listed_lanes[pl.ds(shard, 1), :].astype(F32)
        offset = jnp.sum(jnp.where(diagonal, listed, 0.0), axis=1, keepdims=True)
        position = jnp.where(offset < 0.0, -1.0, offset + (shard * tokens).astype(F32))
        start = pl.multiple_of(shard * rows, 16)
        row_position[pl.ds(start, rows), :] = jnp.broadcast_to(position, (rows, HEAD))
        return carry

    lax.fori_loop(0, shards, fill, 0)

    def place_positions(b, carry):
        lanes = []
        for t in range(0, UNITS, HEAD // UNIT):
            found = []
            for u in range(t, t + HEAD // UNIT):
                code = tiles[b * UNITS + u]
                start = pl.multiple_of((code >> 3) * rows + (code & 7) * UNIT, UNIT)
                found.append(row_position[pl.ds(start, UNIT), :])
            lanes.append(jnp.concatenate(found, axis=0).T[:8])
        positions[b] = jnp.concatenate(lanes + lanes, axis=1).astype(I32)
        return carry

    lax.fori_loop(0, blocks, place_positions, 0)


def plan(page_map, span_order, listed_count, listed_lanes):
    shards, rows = listed_lanes.shape
    smem = pl.BlockSpec(memory_space=SMEM)
    vmem = pl.BlockSpec(memory_space=VMEM)
    pages = page_map.shape[0]
    block_limit = pl.cdiv(shards * (rows // UNIT), UNITS)
    return pl.pallas_call(
        plan_kernel,
        in_specs=[smem, smem, smem, vmem],
        out_specs=[smem, smem, smem, smem, vmem],
        out_shape=[
            jax.ShapeDtypeStruct((pages,), I32),
            jax.ShapeDtypeStruct((pages,), I32),
            jax.ShapeDtypeStruct(((block_limit + 1) * UNITS,), I32),
            jax.ShapeDtypeStruct((1,), I32),
            jax.ShapeDtypeStruct((block_limit, 8, 2 * UNIT * UNITS), I32),
        ],
        scratch_shapes=[pltpu.VMEM((shards * rows, HEAD), F32)],
        compiler_params=params(16),
        cost_estimate=pl.CostEstimate(
            flops=9000000000, bytes_accessed=3000000, transcendentals=0
        ),
        name="plan",
    )(page_map, span_order, listed_count, listed_lanes)


GROUPS = 4


def blend_kernel(
    me_ref, source, place, listed_lanes, received, mine, returned, ordered, blocks, sems
):
    shards, sent, _ = received.shape
    rows = listed_lanes.shape[1]
    own_pages = source.shape[0] // shards
    page_tokens = PAGE
    tokens = own_pages * page_tokens
    part = shards // GROUPS
    per_part = part * tokens // HEAD
    is_key = me_ref[0] % 2 == 0
    flat = received.reshape(shards * sent, HEAD)
    token = lax.broadcasted_iota(I32, (tokens, rows), 0)
    ones = jnp.ones((rows, HEAD), BF16)
    all_ones = jnp.ones((HEAD, HEAD), BF16)

    def send(g):
        span = pl.ds(g * per_part, per_part)
        return pltpu.make_async_copy(blocks.at[span], mine.at[span], sems.at[g])

    def group_step(g, most):
        for u in range(part):
            shard = g * part + u
            pages = []
            for page in range(own_pages):
                start = pl.multiple_of(source[shard * own_pages + page], page_tokens)
                pages.append(flat[pl.ds(start, page_tokens), :])
            cached = jnp.concatenate(pages, axis=0)
            pick = jnp.where(listed_lanes[pl.ds(shard, 1), :] == token, 1.0, 0.0).astype(BF16)
            fresh = jnp.concatenate([received[shard, 2 * rows + tokens :, :], ones], axis=1)
            found = jnp.dot(pick, fresh, preferred_element_type=F32)
            mixed = jnp.where(found[:, HEAD:] > 0.5, found[:, :HEAD], cached.astype(F32))
            start = pl.multiple_of(shard * tokens, 16)
            ordered[pl.ds(start, tokens), :] = mixed.astype(BF16)
            squares = jnp.dot((mixed * mixed).astype(BF16), all_ones, preferred_element_type=F32)
            most = jnp.maximum(most, jnp.max(squares.reshape(tokens // 8, 8, HEAD), axis=0))
        for u in range(per_part):
            at = g * per_part + u
            block = ordered[pl.ds(pl.multiple_of(at * HEAD, HEAD), HEAD), :]
            blocks[at] = jnp.where(is_key, block, block.T)
        send(g).start()
        return most

    most = lax.fori_loop(0, GROUPS, group_step, jnp.zeros((8, HEAD), F32))
    most = jnp.max(most, axis=0, keepdims=True)
    last = GROUPS * per_part
    blocks[last] = jnp.broadcast_to(most, (HEAD, HEAD)).astype(BF16)
    send_last = pltpu.make_async_copy(blocks.at[last], mine.at[last], sems.at[GROUPS])
    send_last.start()

    returned_pages = returned.shape[1] // page_tokens
    first = ((me_ref[0] // 2) % 2) * (own_pages - returned_pages)

    def return_step(shard, carry):
        for page in range(returned_pages):
            start = pl.multiple_of(place[shard * own_pages + first + page], page_tokens)
            span = slice(page * page_tokens, (page + 1) * page_tokens)
            returned[shard, span] = ordered[pl.ds(start, page_tokens), :]
        return carry

    lax.fori_loop(0, shards, return_step, 0, unroll=4)
    for g in range(GROUPS):
        send(g).wait()
    send_last.wait()


def blend(me, source, place, listed_lanes, received):
    shards, rows = listed_lanes.shape
    pages = source.shape[0]
    returned_pages = (pages // shards + 1) // 2
    smem = pl.BlockSpec(memory_space=SMEM)
    vmem = pl.BlockSpec(memory_space=VMEM)
    blocks = (pages * PAGE // HEAD + 1, HEAD, HEAD)
    return pl.pallas_call(
        blend_kernel,
        in_specs=[smem, smem, smem, vmem, vmem],
        out_specs=[pl.BlockSpec(memory_space=OUT_SPACE), vmem],
        out_shape=[
            jax.ShapeDtypeStruct(blocks, BF16),
            jax.ShapeDtypeStruct((shards, returned_pages * PAGE, HEAD), BF16),
        ],
        scratch_shapes=[
            pltpu.VMEM((pages * PAGE, HEAD), BF16),
            pltpu.VMEM(blocks, BF16),
            pltpu.SemaphoreType.DMA((GROUPS + 1,)),
        ],
        compiler_params=params(16),
        cost_estimate=pl.CostEstimate(
            flops=4000000000, bytes_accessed=3000000, transcendentals=0
        ),
        name="blend",
    )(me, source, place, listed_lanes, received)


SLACK = 60.0
LEAST = 2.0**-90


def attend_kernel(
    me_ref, tiles, block_count, positions, received, mine, other, out, block, wide_out
):
    core = me_ref[0] % 2
    wide_out[...] = jnp.zeros_like(wide_out)

    @pl.when(core == 0)
    def _():
        attend_blocks(
            tiles, block_count, positions, received, mine, other, wide_out, block
        )

    @pl.when(core != 0)
    def _():
        attend_blocks(
            tiles, block_count, positions, received, other, mine, wide_out, block
        )

    out[...] = wide_out[...].astype(BF16)


def attend_blocks(
    tiles, block_count, positions, received, keys, values_t, out, block
):
    per_chunk = CHUNK // HEAD
    chunks = keys.shape[0] // per_chunk
    shards = out.shape[0]
    rows = out.shape[1] // 2
    tokens = chunks * CHUNK // shards
    half = UNITS * UNIT
    wide = 2 * half
    top = keys[chunks * per_chunk, :1, :1].astype(F32)
    ones = jnp.ones((16, chunks * CHUNK), BF16)

    def block_step(b, carry):
        first_tile = b * UNITS
        codes = [tiles[first_tile + t] for t in range(UNITS)]
        for t in range(UNITS):
            shard, unit = codes[t] >> 3, codes[t] & 7
            odd = (unit & 1) == 1
            for side in range(2):
                row = pl.multiple_of(side * rows + (unit >> 1) * 16, 16)
                pair = received[shard, pl.ds(row, 16), :].astype(F32)
                at = side * half + t * UNIT
                block[at : at + UNIT] = jnp.where(odd, pair[UNIT:], pair[:UNIT])
        seen_keys = ((codes[UNITS - 1] >> 3) + 1) * tokens
        seen_chunks = (seen_keys + CHUNK - 1) // CHUNK
        query = block[...].astype(BF16)
        position = positions[b][:1]

        def score(start, count):
            products = lax.dot_general(
                keys[pl.ds(start, count)].reshape(count * HEAD, HEAD),
                query,
                (((1,), (1,)), ((), ())),
                preferred_element_type=F32,
            )
            return products * EXP2_SCALE

        def edge_score(start, count):
            found = score(start, count)
            key_position = start * HEAD + lax.broadcasted_iota(I32, (count * HEAD, wide), 0)
            return jnp.where(key_position <= position, found, MASKED)

        def add(start, count, found, shift, state):
            exps = jnp.exp2(found - shift).astype(BF16)
            value = [values_t[start + u] for u in range(count)]
            value = jnp.concatenate([jnp.concatenate(value, axis=1), ones[:, : count * HEAD]], axis=0)
            return state + jnp.dot(value, exps, preferred_element_type=F32)

        def finish(state):
            total = state[HEAD : HEAD + 1]
            result = state[:HEAD] / jnp.where(total > 0, total, 1.0)
            result = jnp.where(position >= 0, result, 0.0).T
            for t in range(UNITS):
                shard, unit = codes[t] >> 3, codes[t] & 7
                for side in range(2):
                    row = pl.multiple_of(side * rows + unit * UNIT, UNIT)
                    at = side * half + t * UNIT
                    out[shard, pl.ds(row, UNIT), :] = result[at : at + UNIT]
            return total

        nothing = jnp.zeros((HEAD + 16, wide), F32)
        squares = query.astype(F32)
        squares = lax.dot_general(
            jnp.ones((8, HEAD), BF16),
            (squares * squares).astype(BF16),
            (((1,), (1,)), ((), ())),
            preferred_element_type=F32,
        )
        bound = jnp.sqrt(squares[:1] * top) * (1.02 * EXP2_SCALE) - SLACK
        def whole(count):
            return lambda: add(0, count, edge_score(0, count), bound, nothing)

        state = lax.switch(
            jnp.maximum(seen_chunks, 1) - 1,
            [whole((c + 1) * per_chunk) for c in range(chunks)],
        )
        total = finish(state)
        lowest = jnp.min(jnp.where(position >= 0, total, 1.0))

        @pl.when(lowest < LEAST)
        def _():
            def keep(chunk, best):
                found = edge_score(chunk * per_chunk, per_chunk)
                return jnp.maximum(best, jnp.max(found.reshape(CHUNK // 8, 8, wide), axis=0))

            best = lax.fori_loop(0, seen_chunks, keep, jnp.full((8, wide), MASKED, F32))
            best = jnp.max(best, axis=0, keepdims=True)

            def again(chunk, st):
                start = chunk * per_chunk
                return add(start, per_chunk, edge_score(start, per_chunk), best, st)

            finish(lax.fori_loop(0, seen_chunks, again, nothing))

        return carry

    lax.fori_loop(0, block_count[0], block_step, 0)


def attend(me, tiles, block_count, positions, received, mine, other, rows):
    shards = received.shape[0]
    smem = pl.BlockSpec(memory_space=SMEM)
    vmem = pl.BlockSpec(memory_space=VMEM)
    block = 2 * UNITS * UNIT
    return pl.pallas_call(
        attend_kernel,
        in_specs=[smem, smem, smem, vmem, vmem, vmem, vmem],
        out_specs=vmem,
        out_shape=jax.ShapeDtypeStruct((shards, 2 * rows, HEAD), BF16),
        scratch_shapes=[
            pltpu.VMEM((block, HEAD), F32),
            pltpu.VMEM((shards, 2 * rows, HEAD), F32),
        ],
        compiler_params=params(32),
        cost_estimate=pl.CostEstimate(
            flops=16000000000, bytes_accessed=3000000, transcendentals=0
        ),
        name="attend",
    )(me, tiles, block_count, positions, received, mine, other)


def place_cache_kernel(received, keys, values):
    own_pages, page_tokens, _ = keys.shape
    shared = received.shape[1] // page_tokens
    for part, target in ((0, keys), (1, values)):
        for page in range(own_pages):
            source, at = (part, page) if page < shared else (2 + part, page - own_pages + shared)
            target[page] = received[source, at * page_tokens : (at + 1) * page_tokens]


def place_cache(received, own_pages, page_tokens):
    shards, sent, _ = received.shape
    group = shards // KV_HEADS
    cache = jax.ShapeDtypeStruct((own_pages, page_tokens, KV_HEADS * HEAD), BF16)
    spec = pl.BlockSpec((own_pages, page_tokens, HEAD), lambda h: (0, 0, h))
    return pl.pallas_call(
        place_cache_kernel,
        grid=(KV_HEADS,),
        in_specs=[pl.BlockSpec((group, sent, HEAD), lambda h: (h, 0, 0))],
        out_specs=[spec, spec],
        out_shape=[cache, cache],
        compiler_params=params(16),
        cost_estimate=pl.CostEstimate(
            flops=2500000000, bytes_accessed=3000000, transcendentals=0
        ),
        name="place_cache",
    )(received)


def place_attended_kernel(received, out, sem):
    rows = out.shape[0]
    for head in range(2 * received.shape[0]):
        row, lane = head % 2 * rows, head * HEAD
        pltpu.make_async_copy(
            received.at[head // 2, pl.ds(row, rows)], out.at[:, pl.ds(lane, HEAD)], sem
        ).start()
    pltpu.make_async_copy(out, out, sem).wait()


def place_attended(received):
    shards, sent, _ = received.shape
    anywhere = pl.BlockSpec(memory_space=pl.ANY)
    return pl.pallas_call(
        place_attended_kernel,
        in_specs=[anywhere],
        out_specs=anywhere,
        out_shape=jax.ShapeDtypeStruct((sent // 2, shards * 2 * HEAD), BF16),
        scratch_shapes=[pltpu.SemaphoreType.DMA],
        compiler_params=params(16),
        cost_estimate=pl.CostEstimate(flops=0, bytes_accessed=1600000, transcendentals=0),
        name="place_attended",
    )(received)


def exchange(blocks):
    return lax.all_to_all(blocks, "shard", 0, 0)


def shard_program(
    shards,
    paged_key_store,
    paged_value_store,
    paged_scale_store,
    page_map,
    span_order,
    listed_count,
    listed_index,
    listed_queries,
    selected_token_keys,
    selected_token_values,
):
    own_pages, page_tokens, _ = paged_key_store.shape
    rows = listed_queries.shape[0]
    me = lax.axis_index("shard").astype(I32).reshape(1)

    received = exchange(
        prepare(
            me,
            page_map,
            span_order,
            listed_index,
            paged_scale_store.transpose(1, 2, 0),
            listed_queries,
            paged_key_store,
            paged_value_store,
            selected_token_keys,
            selected_token_values,
            shards,
        )
    )

    listed = jnp.arange(rows, dtype=I32)[None, :] < listed_count[:, None]
    listed_lanes = jnp.where(listed, listed_index.reshape(shards, rows), -1)
    source, place, tiles, block_count, positions = plan(
        page_map, span_order, listed_count, listed_lanes
    )

    mine, returned = blend(me, source, place, listed_lanes, received)
    other = lax.ppermute(mine, "shard", [(i, i ^ 1) for i in range(shards)])
    received_cache = exchange(returned)
    attended = attend(me, tiles, block_count, positions, received, mine, other, rows)
    mixed_keys, mixed_values = place_cache(received_cache, own_pages, page_tokens)
    return mixed_keys, mixed_values, place_attended(exchange(attended))


def solution(mesh):
    split = ("req", "shard")
    in_specs = (
        P(split, None, None),
        P(split, None, None),
        P(split, None, None),
        P("req"),
        P("req"),
        P("req"),
        P("req"),
        P(split, None),
        P(split, None),
        P(split, None),
    )
    out_specs = (P(split, None, None), P(split, None, None), P(split, None))
    return jax.shard_map(
        functools.partial(shard_program, mesh.shape["shard"]),
        mesh=mesh,
        in_specs=in_specs,
        out_specs=out_specs,
        check_vma=False,
    )
```

```python
import functools

import jax
import jax.numpy as jnp
import numpy as np
from jax import lax
from jax.experimental import pallas as pl
from jax.experimental.pallas import tpu as pltpu
from jax.sharding import PartitionSpec as P

HEAD = 128
KV_HEADS = 8
SPAN_LEN = 704
ROPE_BASE = 1000000.0
MASKED = -1e30
VMEM_MIB = 56
UNIT = 8
UNITS = 32
CHUNK = 1408
PAGE = 16
EXP2_SCALE = float(HEAD**-0.5 / np.log(2.0))

BF16 = jnp.bfloat16
F32 = jnp.float32
I32 = jnp.int32
SMEM = pltpu.SMEM
VMEM = pltpu.VMEM
OUT_SPACE = pltpu.HBM


def rope_frequency():
    half = HEAD // 2
    frequency = ROPE_BASE ** (-(np.arange(half, dtype=np.float64) * 2.0) / HEAD)
    return np.concatenate([frequency, frequency]).astype(np.float32)[None, :]


def rope_tables(position, frequency):
    angles = position * frequency
    lane = lax.broadcasted_iota(I32, angles.shape, 1)
    sine = jnp.sin(angles)
    return jnp.cos(angles), jnp.where(lane < HEAD // 2, -sine, sine)


def rotate(x, cosine, sine):
    return x * cosine + pltpu.roll(x, HEAD // 2, 1) * sine


def params(mib, **more):
    return pltpu.CompilerParams(vmem_limit_bytes=mib * 1024 * 1024, **more)


def prepare_kernel(
    me_ref,
    page_map,
    span_order,
    listed_index,
    scale,
    frequency,
    queries_in,
    keys_in,
    values_in,
    fresh_keys_in,
    fresh_values_in,
    out,
    queries,
    keys,
    values,
    fresh_keys,
    fresh_values,
    blocks,
    slots,
    positions,
    shift_cos,
    shift_sin,
    in_sems,
    out_sems,
):
    me = me_ref[0]
    own_pages, page_tokens, _ = keys.shape
    rows = fresh_keys.shape[0]
    group = blocks.shape[0] // KV_HEADS
    span_count = span_order.shape[0]
    per_span = page_map.shape[0] // span_count
    tokens = own_pages * page_tokens
    arrivals = [
        pltpu.make_async_copy(source, target, in_sems.at[i])
        for i, (source, target) in enumerate(
            (
                (keys_in, keys),
                (values_in, values),
                (fresh_keys_in, fresh_keys),
                (fresh_values_in, fresh_values),
            )
        )
    ]
    query_arrivals = []
    for head in range(KV_HEADS):
        wide = queries.shape[1] // KV_HEADS
        lanes = pl.ds(head * wide, wide)
        query_arrivals.append(
            pltpu.make_async_copy(
                queries_in.at[:, lanes], queries.at[:, lanes], in_sems.at[len(arrivals) + head]
            )
        )
    for arrival in arrivals + query_arrivals:
        arrival.start()

    for c in range(rows):
        position = (me * tokens + listed_index[me * rows + c]).astype(F32)
        positions[c : c + 1, :] = jnp.full((1, HEAD), position, F32)
    cosine, sine = rope_tables(positions[...], frequency[...])
    shift = lax.broadcasted_iota(I32, (span_count, HEAD), 0) * SPAN_LEN
    shift_cos[...], shift_sin[...] = rope_tables(shift.astype(F32), frequency[...])
    first = me * own_pages
    for slot in range(span_count):
        start = span_order[slot] * per_span

        def note(p, carry):
            place = page_map[start + p] - first
            inside = (place >= 0) & (place < own_pages)
            slots[jnp.where(inside, place, own_pages)] = slot
            return carry

        lax.fori_loop(0, per_span, note, 0, unroll=11)
    page_slots = [slots[page] for page in range(own_pages)]
    for arrival in arrivals:
        arrival.wait()

    departures = []
    for head in range(KV_HEADS):
        lanes = slice(head * HEAD, (head + 1) * HEAD)
        outs = [head * group + j for j in range(group)]
        query_arrivals[head].wait()
        for j in range(group):
            for t in range(2):
                at = (2 * (head * group + j) + t) * HEAD
                x = queries[:, at : at + HEAD].astype(F32)
                blocks[outs[j], t * rows : (t + 1) * rows] = rotate(x, cosine, sine).astype(BF16)
        base = 2 * rows
        for page in range(own_pages):
            page_cos = shift_cos[pl.ds(page_slots[page], 1), :]
            page_sin = shift_sin[pl.ds(page_slots[page], 1), :]
            span = slice(base + page * page_tokens, base + (page + 1) * page_tokens)
            key = keys[page, :, lanes].astype(F32) * scale[0, head, page]
            key = rotate(key, page_cos, page_sin).astype(BF16)
            value = (values[page, :, lanes].astype(F32) * scale[1, head, page]).astype(BF16)
            for j in range(group):
                blocks[outs[j], span] = value if j % 2 else key
        key = rotate(fresh_keys[:, lanes].astype(F32), cosine, sine).astype(BF16)
        value = fresh_values[:, lanes]
        for j in range(group):
            blocks[outs[j], base + tokens :] = value if j % 2 else key
        span = pl.ds(head * group, group)
        departures.append(
            pltpu.make_async_copy(blocks.at[span], out.at[span], out_sems.at[head])
        )
        departures[-1].start()
    for departure in departures:
        departure.wait()


def prepare(
    me,
    page_map,
    span_order,
    listed_index,
    scale,
    queries,
    keys,
    values,
    fresh_keys,
    fresh_values,
    shards,
):
    own_pages, page_tokens, _ = keys.shape
    rows, width = queries.shape
    sent = 3 * rows + own_pages * page_tokens
    smem = pl.BlockSpec(memory_space=SMEM)
    vmem = pl.BlockSpec(memory_space=VMEM)
    anywhere = pl.BlockSpec(memory_space=pl.ANY)
    arrays = (queries, keys, values, fresh_keys, fresh_values)
    return pl.pallas_call(
        prepare_kernel,
        in_specs=[smem] * 5 + [vmem] + [anywhere] * 5,
        out_specs=pl.BlockSpec(memory_space=OUT_SPACE),
        out_shape=jax.ShapeDtypeStruct((shards, sent, HEAD), BF16),
        scratch_shapes=[pltpu.VMEM(a.shape, a.dtype) for a in arrays]
        + [
            pltpu.VMEM((shards, sent, HEAD), BF16),
            pltpu.SMEM((own_pages + 1,), I32),
            pltpu.VMEM((rows, HEAD), F32),
            pltpu.VMEM((span_order.shape[0], HEAD), F32),
            pltpu.VMEM((span_order.shape[0], HEAD), F32),
            pltpu.SemaphoreType.DMA((len(arrays) - 1 + KV_HEADS,)),
            pltpu.SemaphoreType.DMA((KV_HEADS,)),
        ],
        compiler_params=params(VMEM_MIB),
        cost_estimate=pl.CostEstimate(
            flops=5000000000, bytes_accessed=4300000, transcendentals=0
        ),
        name="prepare",
    )(
        me,
        page_map,
        span_order,
        listed_index,
        scale,
        jnp.asarray(rope_frequency()),
        *arrays,
    )


def plan_kernel(
    page_map,
    span_order,
    listed_count,
    listed_lanes,
    source,
    place,
    tiles,
    block_count,
    positions,
    row_position,
):
    shards, rows = listed_lanes.shape
    pages = page_map.shape[0]
    own_pages = pages // shards
    page_tokens = PAGE
    tokens = own_pages * page_tokens
    sent = tokens + 3 * rows
    span_count = span_order.shape[0]
    per_span = pages // span_count

    for slot in range(span_count):
        start = span_order[slot] * per_span

        def note(p, carry):
            stored = page_map[start + p]
            logical = slot * per_span + p
            owner = stored // own_pages
            within = stored - owner * own_pages
            source[logical] = owner * sent + 2 * rows + within * page_tokens
            place[stored] = logical * page_tokens
            return carry

        lax.fori_loop(0, per_span, note, 0, unroll=4)

    def count_tiles(shard, total):
        return total + (listed_count[shard] + UNIT - 1) // UNIT

    total = lax.fori_loop(0, shards, count_tiles, 0)
    blocks = (total + UNITS - 1) // UNITS
    block_count[0] = blocks
    for k in range(UNITS):
        tiles[k] = 0

    def list_tiles(shard, filled):
        count = listed_count[shard]
        for k in range(rows // UNIT):
            tiles[filled] = shard * 8 + k
            filled = filled + jnp.where(count > UNIT * k, 1, 0)
        return filled

    lax.fori_loop(0, shards, list_tiles, blocks * UNITS - total)

    diagonal = lax.broadcasted_iota(I32, (rows, rows), 0) == lax.broadcasted_iota(
        I32, (rows, rows), 1
    )

    def fill(shard, carry):
        listed = listed_lanes[pl.ds(shard, 1), :].astype(F32)
        offset = jnp.sum(jnp.where(diagonal, listed, 0.0), axis=1, keepdims=True)
        position = jnp.where(offset < 0.0, -1.0, offset + (shard * tokens).astype(F32))
        start = pl.multiple_of(shard * rows, 16)
        row_position[pl.ds(start, rows), :] = jnp.broadcast_to(position, (rows, HEAD))
        return carry

    lax.fori_loop(0, shards, fill, 0)

    def place_positions(b, carry):
        lanes = []
        for t in range(0, UNITS, HEAD // UNIT):
            found = []
            for u in range(t, t + HEAD // UNIT):
                code = tiles[b * UNITS + u]
                start = pl.multiple_of((code >> 3) * rows + (code & 7) * UNIT, UNIT)
                found.append(row_position[pl.ds(start, UNIT), :])
            lanes.append(jnp.concatenate(found, axis=0).T[:8])
        positions[b] = jnp.concatenate(lanes + lanes, axis=1).astype(I32)
        return carry

    lax.fori_loop(0, blocks, place_positions, 0)


def plan(page_map, span_order, listed_count, listed_lanes):
    shards, rows = listed_lanes.shape
    smem = pl.BlockSpec(memory_space=SMEM)
    vmem = pl.BlockSpec(memory_space=VMEM)
    pages = page_map.shape[0]
    block_limit = pl.cdiv(shards * (rows // UNIT), UNITS)
    return pl.pallas_call(
        plan_kernel,
        in_specs=[smem, smem, smem, vmem],
        out_specs=[smem, smem, smem, smem, vmem],
        out_shape=[
            jax.ShapeDtypeStruct((pages,), I32),
            jax.ShapeDtypeStruct((pages,), I32),
            jax.ShapeDtypeStruct(((block_limit + 1) * UNITS,), I32),
            jax.ShapeDtypeStruct((1,), I32),
            jax.ShapeDtypeStruct((block_limit, 8, 2 * UNIT * UNITS), I32),
        ],
        scratch_shapes=[pltpu.VMEM((shards * rows, HEAD), F32)],
        compiler_params=params(16),
        cost_estimate=pl.CostEstimate(
            flops=9000000000, bytes_accessed=3000000, transcendentals=0
        ),
        name="plan",
    )(page_map, span_order, listed_count, listed_lanes)


GROUPS = 2


def blend_kernel(
    me_ref, source, place, listed_lanes, received, mine, returned, ordered, blocks, sems
):
    shards, sent, _ = received.shape
    rows = listed_lanes.shape[1]
    own_pages = source.shape[0] // shards
    page_tokens = PAGE
    tokens = own_pages * page_tokens
    part = shards // GROUPS
    per_part = part * tokens // HEAD
    is_key = me_ref[0] % 2 == 0
    flat = received.reshape(shards * sent, HEAD)
    token = lax.broadcasted_iota(I32, (tokens, rows), 0)
    ones = jnp.ones((rows, HEAD), BF16)
    all_ones = jnp.ones((HEAD, HEAD), BF16)

    def send(g):
        span = pl.ds(g * per_part, per_part)
        return pltpu.make_async_copy(blocks.at[span], mine.at[span], sems.at[g])

    def group_step(g, most):
        for u in range(part):
            shard = g * part + u
            pages = []
            for page in range(own_pages):
                start = pl.multiple_of(source[shard * own_pages + page], page_tokens)
                pages.append(flat[pl.ds(start, page_tokens), :])
            cached = jnp.concatenate(pages, axis=0)
            pick = jnp.where(listed_lanes[pl.ds(shard, 1), :] == token, 1.0, 0.0).astype(BF16)
            fresh = jnp.concatenate([received[shard, 2 * rows + tokens :, :], ones], axis=1)
            found = jnp.dot(pick, fresh, preferred_element_type=F32)
            mixed = jnp.where(found[:, HEAD:] > 0.5, found[:, :HEAD], cached.astype(F32))
            start = pl.multiple_of(shard * tokens, 16)
            ordered[pl.ds(start, tokens), :] = mixed.astype(BF16)
            squares = jnp.dot((mixed * mixed).astype(BF16), all_ones, preferred_element_type=F32)
            most = jnp.maximum(most, jnp.max(squares.reshape(tokens // 8, 8, HEAD), axis=0))
        for u in range(per_part):
            at = g * per_part + u
            block = ordered[pl.ds(pl.multiple_of(at * HEAD, HEAD), HEAD), :]
            blocks[at] = jnp.where(is_key, block, block.T)
        send(g).start()
        return most

    most = lax.fori_loop(0, GROUPS, group_step, jnp.zeros((8, HEAD), F32))
    most = jnp.max(most, axis=0, keepdims=True)
    last = GROUPS * per_part
    blocks[last] = jnp.broadcast_to(most, (HEAD, HEAD)).astype(BF16)
    send_last = pltpu.make_async_copy(blocks.at[last], mine.at[last], sems.at[GROUPS])
    send_last.start()

    returned_pages = returned.shape[1] // page_tokens
    first = ((me_ref[0] // 2) % 2) * (own_pages - returned_pages)

    def return_step(shard, carry):
        for page in range(returned_pages):
            start = pl.multiple_of(place[shard * own_pages + first + page], page_tokens)
            span = slice(page * page_tokens, (page + 1) * page_tokens)
            returned[shard, span] = ordered[pl.ds(start, page_tokens), :]
        return carry

    lax.fori_loop(0, shards, return_step, 0, unroll=4)
    for g in range(GROUPS):
        send(g).wait()
    send_last.wait()


def blend(me, source, place, listed_lanes, received):
    shards, rows = listed_lanes.shape
    pages = source.shape[0]
    returned_pages = (pages // shards + 1) // 2
    smem = pl.BlockSpec(memory_space=SMEM)
    vmem = pl.BlockSpec(memory_space=VMEM)
    blocks = (pages * PAGE // HEAD + 1, HEAD, HEAD)
    return pl.pallas_call(
        blend_kernel,
        in_specs=[smem, smem, smem, vmem, vmem],
        out_specs=[pl.BlockSpec(memory_space=OUT_SPACE), vmem],
        out_shape=[
            jax.ShapeDtypeStruct(blocks, BF16),
            jax.ShapeDtypeStruct((shards, returned_pages * PAGE, HEAD), BF16),
        ],
        scratch_shapes=[
            pltpu.VMEM((pages * PAGE, HEAD), BF16),
            pltpu.VMEM(blocks, BF16),
            pltpu.SemaphoreType.DMA((GROUPS + 1,)),
        ],
        compiler_params=params(16),
        cost_estimate=pl.CostEstimate(
            flops=4000000000, bytes_accessed=3000000, transcendentals=0
        ),
        name="blend",
    )(me, source, place, listed_lanes, received)


SLACK = 60.0
LEAST = 2.0**-90


def attend_kernel(
    me_ref, tiles, block_count, positions, received, mine, other, out, block, wide_out
):
    core = me_ref[0] % 2
    wide_out[...] = jnp.zeros_like(wide_out)

    @pl.when(core == 0)
    def _():
        attend_blocks(
            tiles, block_count, positions, received, mine, other, wide_out, block
        )

    @pl.when(core != 0)
    def _():
        attend_blocks(
            tiles, block_count, positions, received, other, mine, wide_out, block
        )

    out[...] = wide_out[...].astype(BF16)


def attend_blocks(
    tiles, block_count, positions, received, keys, values_t, out, block
):
    per_chunk = CHUNK // HEAD
    chunks = keys.shape[0] // per_chunk
    shards = out.shape[0]
    rows = out.shape[1] // 2
    tokens = chunks * CHUNK // shards
    half = UNITS * UNIT
    wide = 2 * half
    top = keys[chunks * per_chunk, :1, :1].astype(F32)
    ones = jnp.ones((16, chunks * CHUNK), BF16)

    def block_step(b, carry):
        first_tile = b * UNITS
        codes = [tiles[first_tile + t] for t in range(UNITS)]
        for t in range(UNITS):
            shard, unit = codes[t] >> 3, codes[t] & 7
            odd = (unit & 1) == 1
            for side in range(2):
                row = pl.multiple_of(side * rows + (unit >> 1) * 16, 16)
                pair = received[shard, pl.ds(row, 16), :].astype(F32)
                at = side * half + t * UNIT
                block[at : at + UNIT] = jnp.where(odd, pair[UNIT:], pair[:UNIT])
        seen_keys = ((codes[UNITS - 1] >> 3) + 1) * tokens
        seen_chunks = (seen_keys + CHUNK - 1) // CHUNK
        query = block[...].astype(BF16)
        position = positions[b][:1]

        def score(start, count):
            products = lax.dot_general(
                keys[pl.ds(start, count)].reshape(count * HEAD, HEAD),
                query,
                (((1,), (1,)), ((), ())),
                preferred_element_type=F32,
            )
            return products * EXP2_SCALE

        def edge_score(start, count):
            found = score(start, count)
            key_position = start * HEAD + lax.broadcasted_iota(I32, (count * HEAD, wide), 0)
            return jnp.where(key_position <= position, found, MASKED)

        def add(start, count, found, shift, state):
            exps = jnp.exp2(found - shift).astype(BF16)
            value = [values_t[start + u] for u in range(count)]
            value = jnp.concatenate([jnp.concatenate(value, axis=1), ones[:, : count * HEAD]], axis=0)
            return state + jnp.dot(value, exps, preferred_element_type=F32)

        def finish(state):
            total = state[HEAD : HEAD + 1]
            result = state[:HEAD] / jnp.where(total > 0, total, 1.0)
            result = jnp.where(position >= 0, result, 0.0).T
            for t in range(UNITS):
                shard, unit = codes[t] >> 3, codes[t] & 7
                for side in range(2):
                    row = pl.multiple_of(side * rows + unit * UNIT, UNIT)
                    at = side * half + t * UNIT
                    out[shard, pl.ds(row, UNIT), :] = result[at : at + UNIT]
            return total

        nothing = jnp.zeros((HEAD + 16, wide), F32)
        squares = query.astype(F32)
        squares = lax.dot_general(
            jnp.ones((8, HEAD), BF16),
            (squares * squares).astype(BF16),
            (((1,), (1,)), ((), ())),
            preferred_element_type=F32,
        )
        bound = jnp.sqrt(squares[:1] * top) * (1.02 * EXP2_SCALE) - SLACK
        def whole(count):
            return lambda: add(0, count, edge_score(0, count), bound, nothing)

        state = lax.switch(
            jnp.maximum(seen_chunks, 1) - 1,
            [whole((c + 1) * per_chunk) for c in range(chunks)],
        )
        total = finish(state)
        lowest = jnp.min(jnp.where(position >= 0, total, 1.0))

        @pl.when(lowest < LEAST)
        def _():
            def keep(chunk, best):
                found = edge_score(chunk * per_chunk, per_chunk)
                return jnp.maximum(best, jnp.max(found.reshape(CHUNK // 8, 8, wide), axis=0))

            best = lax.fori_loop(0, seen_chunks, keep, jnp.full((8, wide), MASKED, F32))
            best = jnp.max(best, axis=0, keepdims=True)

            def again(chunk, st):
                start = chunk * per_chunk
                return add(start, per_chunk, edge_score(start, per_chunk), best, st)

            finish(lax.fori_loop(0, seen_chunks, again, nothing))

        return carry

    lax.fori_loop(0, block_count[0], block_step, 0)


def attend(me, tiles, block_count, positions, received, mine, other, rows):
    shards = received.shape[0]
    smem = pl.BlockSpec(memory_space=SMEM)
    vmem = pl.BlockSpec(memory_space=VMEM)
    block = 2 * UNITS * UNIT
    return pl.pallas_call(
        attend_kernel,
        in_specs=[smem, smem, smem, vmem, vmem, vmem, vmem],
        out_specs=vmem,
        out_shape=jax.ShapeDtypeStruct((shards, 2 * rows, HEAD), BF16),
        scratch_shapes=[
            pltpu.VMEM((block, HEAD), F32),
            pltpu.VMEM((shards, 2 * rows, HEAD), F32),
        ],
        compiler_params=params(32),
        cost_estimate=pl.CostEstimate(
            flops=16000000000, bytes_accessed=3000000, transcendentals=0
        ),
        name="attend",
    )(me, tiles, block_count, positions, received, mine, other)


def place_cache_kernel(received, keys, values):
    own_pages, page_tokens, _ = keys.shape
    shared = received.shape[1] // page_tokens
    for part, target in ((0, keys), (1, values)):
        for page in range(own_pages):
            source, at = (part, page) if page < shared else (2 + part, page - own_pages + shared)
            target[page] = received[source, at * page_tokens : (at + 1) * page_tokens]


def place_cache(received, own_pages, page_tokens):
    shards, sent, _ = received.shape
    group = shards // KV_HEADS
    cache = jax.ShapeDtypeStruct((own_pages, page_tokens, KV_HEADS * HEAD), BF16)
    spec = pl.BlockSpec((own_pages, page_tokens, HEAD), lambda h: (0, 0, h))
    return pl.pallas_call(
        place_cache_kernel,
        grid=(KV_HEADS,),
        in_specs=[pl.BlockSpec((group, sent, HEAD), lambda h: (h, 0, 0))],
        out_specs=[spec, spec],
        out_shape=[cache, cache],
        compiler_params=params(16),
        cost_estimate=pl.CostEstimate(
            flops=2500000000, bytes_accessed=3000000, transcendentals=0
        ),
        name="place_cache",
    )(received)


def place_attended_kernel(received, out, sem):
    rows = out.shape[0]
    for head in range(2 * received.shape[0]):
        row, lane = head % 2 * rows, head * HEAD
        pltpu.make_async_copy(
            received.at[head // 2, pl.ds(row, rows)], out.at[:, pl.ds(lane, HEAD)], sem
        ).start()
    pltpu.make_async_copy(out, out, sem).wait()


def place_attended(received):
    shards, sent, _ = received.shape
    anywhere = pl.BlockSpec(memory_space=pl.ANY)
    return pl.pallas_call(
        place_attended_kernel,
        in_specs=[anywhere],
        out_specs=anywhere,
        out_shape=jax.ShapeDtypeStruct((sent // 2, shards * 2 * HEAD), BF16),
        scratch_shapes=[pltpu.SemaphoreType.DMA],
        compiler_params=params(16),
        cost_estimate=pl.CostEstimate(flops=0, bytes_accessed=1600000, transcendentals=0),
        name="place_attended",
    )(received)


def exchange(blocks):
    return lax.all_to_all(blocks, "shard", 0, 0)


def shard_program(
    shards,
    paged_key_store,
    paged_value_store,
    paged_scale_store,
    page_map,
    span_order,
    listed_count,
    listed_index,
    listed_queries,
    selected_token_keys,
    selected_token_values,
):
    own_pages, page_tokens, _ = paged_key_store.shape
    rows = listed_queries.shape[0]
    me = lax.axis_index("shard").astype(I32).reshape(1)

    received = exchange(
        prepare(
            me,
            page_map,
            span_order,
            listed_index,
            paged_scale_store.transpose(1, 2, 0),
            listed_queries,
            paged_key_store,
            paged_value_store,
            selected_token_keys,
            selected_token_values,
            shards,
        )
    )

    listed = jnp.arange(rows, dtype=I32)[None, :] < listed_count[:, None]
    listed_lanes = jnp.where(listed, listed_index.reshape(shards, rows), -1)
    source, place, tiles, block_count, positions = plan(
        page_map, span_order, listed_count, listed_lanes
    )

    mine, returned = blend(me, source, place, listed_lanes, received)
    other = lax.ppermute(mine, "shard", [(i, i ^ 1) for i in range(shards)])
    received_cache = exchange(returned)
    attended = attend(me, tiles, block_count, positions, received, mine, other, rows)
    mixed_keys, mixed_values = place_cache(received_cache, own_pages, page_tokens)
    return mixed_keys, mixed_values, place_attended(exchange(attended))


def solution(mesh):
    split = ("req", "shard")
    in_specs = (
        P(split, None, None),
        P(split, None, None),
        P(split, None, None),
        P("req"),
        P("req"),
        P("req"),
        P("req"),
        P(split, None),
        P(split, None),
        P(split, None),
    )
    out_specs = (P(split, None, None), P(split, None, None), P(split, None))
    return jax.shard_map(
        functools.partial(shard_program, mesh.shape["shard"]),
        mesh=mesh,
        in_specs=in_specs,
        out_specs=out_specs,
        check_vma=False,
    )
```
